256 devices in a mesh: pipe: 8 (over z_lo, x), tensor: 8 (over z_hi, core), dp: 4 (over y).
Axes of the slice: x: 4, y: 4, z: 8 (z_hi: 4, z_lo: 2; z = z_hi * 2 + z_lo), core: 2. Of those that a mesh axis runs over, the one named last changes fastest.
Arguments:
- act: bfloat16 [8, 4, 512, 4096], P('pipe', 'dp', 'tensor'), may hold values from -6 to 6
- direction: int32 [8, 4], P(None, 'dp'), may hold values from 0 to 1
- positions: int32 [8, 4, 512], P('pipe', 'dp'), may hold values from 0 to 511, as said below
- w_query: bfloat16 [8, 4096, 32, 128], P('pipe', 'dp', 'tensor'), may hold values from -0.09375 to 0.09375
- w_keyval: bfloat16 [8, 4096, 8, 2, 128], P('pipe', 'dp', 'tensor'), may hold values from -0.09375 to 0.09375
- out_grad: bfloat16 [8, 4, 512, 32, 128], P('pipe', 'dp', None, 'tensor'), may hold values from -6 to 6
Outputs:
- attn_out: bfloat16 [8, 4, 512, 32, 128], P('pipe', 'dp', None, 'tensor')
- grad_input: bfloat16 [8, 4, 512, 4096], P('pipe', 'dp', 'tensor')
- grad_query: float32 [8, 4096, 32, 128], P('pipe', 'dp', 'tensor')
- grad_keyval: float32 [8, 4096, 8, 2, 128], P('pipe', 'dp', 'tensor')
The draws below stay inside these ranges and needn't reach their ends.
Inputs may be any that keep to these rules, and one draw needn't show every extreme that they name: Each micro-batch's positions are a permutation of 0 to 511.
All inputs are finite; a program needn't handle non-finite values.
Results may differ from the reference program's by a relative error of at most 0.035.
Values may be sent and summed in bfloat16 or wider, within the bound.
No kernel may reach another device: no remote copies, remote signals or barrier semaphores. Data moves between devices by JAX's collectives and lax.ppermute only.
A program may use at most 128 MiB of HBM per device.

```python
import math
import jax
import jax.numpy as jnp
from jax import lax

MODEL_FEATURES = 4096
HQ = 32
KEY_VALUE_HEADS = 8
HEAD_WIDTH = 128
MICRO_TOKENS = 512
RELAY_SECTIONS = 8
REPLICAS = 4
N_TENSOR = 8


def token_order(key):
    order_key = jax.random.fold_in(key, 701)
    stream_keys = jax.random.split(order_key, RELAY_SECTIONS * REPLICAS)

    def one_order(single_key):
        return jax.random.permutation(single_key, MICRO_TOKENS)
    shuffled = jax.vmap(one_order)(stream_keys)
    return shuffled.reshape(RELAY_SECTIONS, REPLICAS, MICRO_TOKENS).astype(jnp.int32)


def draw_positions(key, part):
    return token_order(key)


def draw_act(key, part):
    key = jax.random.fold_in(key, 3)
    complete_shape = (RELAY_SECTIONS, REPLICAS, MICRO_TOKENS, MODEL_FEATURES)
    return jax.random.truncated_normal(key, -6.0, 6.0, complete_shape, jnp.float32).astype(jnp.bfloat16)


def draw_w_query(key, part):
    key = jax.random.fold_in(key, 5)
    complete_shape = (RELAY_SECTIONS, MODEL_FEATURES, HQ, HEAD_WIDTH)
    return (jax.random.truncated_normal(key, -6.0, 6.0, complete_shape, jnp.float32) / math.sqrt(MODEL_FEATURES)).astype(jnp.bfloat16)


def draw_w_keyval(key, part):
    key = jax.random.fold_in(key, 7)
    complete_shape = (RELAY_SECTIONS, MODEL_FEATURES, KEY_VALUE_HEADS, 2, HEAD_WIDTH)
    return (jax.random.truncated_normal(key, -6.0, 6.0, complete_shape, jnp.float32) / math.sqrt(MODEL_FEATURES)).astype(jnp.bfloat16)


def with_ends(array, own_key, low, largest):
    longest = array.shape.index(max(array.shape))
    spots = []
    for shift in (0, 1):
        where = [jax.random.randint(jax.random.fold_in(own_key, axis), (), 0, length) for axis, length in enumerate(array.shape)]
        where[longest] = (where[longest] + shift) % array.shape[longest]
        spots.append(tuple(where))
    return array.at[spots[0]].set(low).at[spots[1]].set(largest)


def steps_of(key, extent, cuts, low, top_value):
    factor_of = 1.0
    for position, shards_of in cuts:
        draws = jax.random.uniform(jax.random.fold_in(jax.random.fold_in(key, 6), position), (shards_of,), jnp.float32, low / len(cuts), top_value / len(cuts))
        factor_of = factor_of * jnp.repeat(jnp.exp(draws), extent[position] // shards_of).reshape((-1,) + (1,) * (len(extent) - 1 - position))
    return factor_of


def centred(rng, shape, width, bound, cuts=(), kind=jnp.bfloat16):
    drawn = width * jax.random.normal(rng, shape, jnp.float32)
    if cuts:
        drawn = drawn * steps_of(rng, shape, cuts, -0.22, 0.18)
    return jnp.clip(drawn, -bound, bound).astype(kind)


def setup_inputs(seed: int = 0) -> dict:
    seeds = jax.random.split(jax.random.key(seed), 7)
    return {
        "act": draw_act(jax.random.fold_in(seeds[6], 71), 0),
        "direction": with_ends(jax.random.randint(seeds[1], (RELAY_SECTIONS, REPLICAS), 0, 2), jax.random.fold_in(seeds[1], 1), 0, 1).astype(jnp.int32),
        "positions": draw_positions(jax.random.fold_in(seeds[6], 71), 0),
        "w_query": draw_w_query(jax.random.fold_in(seeds[6], 71), 0),
        "w_keyval": draw_w_keyval(jax.random.fold_in(seeds[6], 71), 0),
        "out_grad": centred(seeds[5], (RELAY_SECTIONS, REPLICAS, MICRO_TOKENS, HQ, HEAD_WIDTH), 1.0, 6.0, ((0, 8), (1, 4), (3, 8))),
    }


def soft_quantize(weight):
    in_rows = weight.shape[0]
    groups = weight.astype(jnp.float32).reshape(in_rows // 128, 128, -1)
    group_scale = (lax.optimization_barrier(jnp.max(jnp.abs(groups), axis=1, keepdims=True)) + 1e-06) / 7.0
    scaled = groups / group_scale
    stepped = scaled - jnp.sin(2.0 * math.pi * scaled) / (2.0 * math.pi)
    return (group_scale * stepped).reshape(in_rows, -1).astype(jnp.bfloat16)

def rotate(vectors, token_pos):
    half_dim = vectors.shape[-1] // 2
    inv_freq = 1000000.0 ** (-jnp.arange(half_dim, dtype=jnp.float32) / half_dim)
    angles = token_pos.astype(jnp.float32)[:, None] * inv_freq[None, :]
    cosine = jnp.cos(angles)[:, None, :]
    sin_part = jnp.sin(angles)[:, None, :]
    front_half = vectors[..., :half_dim]
    back_half = vectors[..., half_dim:]
    return jnp.concatenate([front_half * cosine - back_half * sin_part, back_half * cosine + front_half * sin_part], axis=-1)

def attend(queries, keys_in, values_in, token_pos):
    length, head_count, head_dim = queries.shape
    kv_count = keys_in.shape[1]
    group_size = head_count // kv_count
    q_rot = rotate(queries.astype(jnp.float32), token_pos).astype(jnp.bfloat16)
    k_rot = rotate(keys_in.astype(jnp.float32), token_pos).astype(jnp.bfloat16)
    grouped = q_rot.reshape(length, kv_count, group_size, head_dim)
    scores = jnp.einsum('skgd,tkd->kgst', grouped.astype(jnp.float32), k_rot.astype(jnp.float32)) / math.sqrt(head_dim)
    visible = token_pos[None, :] <= token_pos[:, None]
    scores = jnp.where(visible, scores, -1e+30)
    row_max = lax.optimization_barrier(jnp.max(scores, axis=-1, keepdims=True))
    raised = jnp.exp(scores - row_max)
    weights = (raised / lax.optimization_barrier(jnp.sum(raised, axis=-1, keepdims=True))).astype(jnp.bfloat16)
    blended = jnp.einsum('kgst,tkd->skgd', weights.astype(jnp.float32), values_in.astype(jnp.float32))
    return blended.reshape(length, head_count, head_dim).astype(jnp.bfloat16)

def reference(act, direction, positions, w_query, w_keyval, out_grad):
    query_columns = HQ * HEAD_WIDTH
    key_value_columns = KEY_VALUE_HEADS * 2 * HEAD_WIDTH
    attn_list = []
    input_list = []
    grad_list = []
    for section_idx in range(RELAY_SECTIONS):
        down_src = act[section_idx] if section_idx == 0 else act[section_idx - 1]
        up_src = act[section_idx] if section_idx == RELAY_SECTIONS - 1 else act[section_idx + 1]
        inputs = jnp.where((direction[section_idx] == 0)[:, None, None], down_src, up_src)
        q_weight = soft_quantize(w_query[section_idx].reshape(MODEL_FEATURES, query_columns))
        kv_weight = soft_quantize(w_keyval[section_idx].reshape(MODEL_FEATURES, key_value_columns))
        combined = jnp.concatenate([q_weight, kv_weight], axis=1)
        grouped_w = jnp.concatenate([q_weight.reshape(MODEL_FEATURES, N_TENSOR, -1), kv_weight.reshape(MODEL_FEATURES, N_TENSOR, -1)], axis=2).astype(jnp.float32)
        proj_grads = []
        for replica in range(REPLICAS):
            tokens = inputs[replica]
            projected_rows = jnp.dot(tokens, combined, preferred_element_type=jnp.float32).astype(jnp.bfloat16)
            queries = projected_rows[:, :query_columns].reshape(MICRO_TOKENS, HQ, HEAD_WIDTH)
            key_value_rows = projected_rows[:, query_columns:].reshape(MICRO_TOKENS, KEY_VALUE_HEADS, 2, HEAD_WIDTH)
            pos_row = positions[section_idx, replica]

            def local_attend(q_in, k_in, v_in):
                return attend(q_in, k_in, v_in, pos_row)
            attended, pull_back = jax.vjp(local_attend, queries, key_value_rows[:, :, 0], key_value_rows[:, :, 1])
            d_query, d_keys, d_values = pull_back(out_grad[section_idx, replica])
            d_keyval = jnp.stack([d_keys, d_values], axis=2)
            d_grouped = jnp.concatenate([d_query.reshape(MICRO_TOKENS, N_TENSOR, -1), d_keyval.reshape(MICRO_TOKENS, N_TENSOR, -1)], axis=2)
            partial_rows = jnp.einsum('stc,dtc->tsd', d_grouped.astype(jnp.float32), grouped_w)
            partial_rows = lax.optimization_barrier(partial_rows.astype(jnp.bfloat16)).astype(jnp.float32)
            input_list.append(lax.optimization_barrier(jnp.sum(partial_rows, axis=0)).astype(jnp.bfloat16))
            proj_grads.append(jnp.concatenate([d_query.reshape(MICRO_TOKENS, query_columns), d_keyval.reshape(MICRO_TOKENS, key_value_columns)], axis=1))
            attn_list.append(attended)
        all_tokens = inputs.reshape(REPLICAS * MICRO_TOKENS, MODEL_FEATURES)
        all_grads = jnp.concatenate(proj_grads, axis=0)
        section_grad = lax.dot_general(all_tokens, all_grads, (((0,), (0,)), ((), ())), preferred_element_type=jnp.float32)
        grad_list.append(section_grad.astype(jnp.bfloat16))
    query_list = []
    key_value_pieces = []
    for section_idx in range(RELAY_SECTIONS):
        own_grad = lax.optimization_barrier(grad_list[section_idx]).astype(jnp.float32)
        far_grad = lax.optimization_barrier(grad_list[RELAY_SECTIONS - 1 - section_idx]).astype(jnp.float32)
        gradient_overall = own_grad + far_grad
        query_list.append(gradient_overall[:, :query_columns].reshape(MODEL_FEATURES, HQ, HEAD_WIDTH))
        key_value_pieces.append(gradient_overall[:, query_columns:].reshape(MODEL_FEATURES, KEY_VALUE_HEADS, 2, HEAD_WIDTH))
    attn_out = jnp.stack(attn_list).reshape(RELAY_SECTIONS, REPLICAS, MICRO_TOKENS, HQ, HEAD_WIDTH)
    grad_input = jnp.stack(input_list).reshape(RELAY_SECTIONS, REPLICAS, MICRO_TOKENS, MODEL_FEATURES)
    return (attn_out, grad_input, jnp.stack(query_list), jnp.stack(key_value_pieces))
```

```python
import functools
import math

import jax
import jax.numpy as jnp
from jax import lax
from jax.experimental import pallas as pl
from jax.experimental.pallas import tpu as pltpu
from jax.sharding import PartitionSpec as P

BF = jnp.bfloat16
F32 = jnp.float32
GROUP = 128


def sin_turns(r):
    a = jnp.abs(r)
    m = jnp.minimum(a, 0.5 - a)
    x = (2.0 * math.pi) * m
    y = x * x
    p = -1.0 / 39916800.0
    p = p * y + 1.0 / 362880.0
    p = p * y - 1.0 / 5040.0
    p = p * y + 1.0 / 120.0
    p = p * y - 1.0 / 6.0
    s = x + x * (y * p)
    return jnp.where(r < 0, -s, s)


def quantize_block(w):
    top = jnp.max(jnp.abs(w), axis=0, keepdims=True)
    scale = (top + 1e-06) / 7.0
    t = w * (1.0 / scale)
    wave = sin_turns(t - jnp.round(t))
    return scale * (t - wave * (1.0 / (2.0 * math.pi)))


def quantize_kernel(wq_ref, wkv_ref, out_ref):
    columns = wq_ref.shape[1]
    out_ref[:, :columns] = quantize_block(wq_ref[...].astype(F32)).astype(BF)
    out_ref[:, columns:] = quantize_block(wkv_ref[...].astype(F32)).astype(BF)


def quantize(w_query, w_keyval):
    rows, q_cols = w_query.shape
    kv_cols = w_keyval.shape[1]
    cols = q_cols + kv_cols
    return pl.pallas_call(
        quantize_kernel,
        grid=(rows // GROUP,),
        in_specs=[
            pl.BlockSpec((GROUP, q_cols), lambda i: (i, 0)),
            pl.BlockSpec((GROUP, kv_cols), lambda i: (i, 0)),
        ],
        out_specs=pl.BlockSpec((GROUP, cols), lambda i: (i, 0)),
        out_shape=jax.ShapeDtypeStruct((rows, cols), BF),
        compiler_params=pltpu.CompilerParams(vmem_limit_bytes=16 * 2**20),
        cost_estimate=pl.CostEstimate(
            flops=30 * rows * cols, bytes_accessed=4 * rows * cols, transcendentals=0
        ),
    )(w_query, w_keyval)


def dot(a, b, dims):
    return lax.dot_general(a, b, (dims, ((), ())), preferred_element_type=F32)


def attention_kernel(
    q_ref, kv_ref, cos_ref, sin_ref, pos_row_ref, pos_col_ref, og_ref,
    out_ref, dq_ref, dkv_ref, k_rot, dk_sum, dv_sum,
):
    width = cos_ref.shape[1]
    half = width // 2
    head = pl.program_id(0)
    heads = pl.num_programs(0)
    cosine = cos_ref[...]
    signed = sin_ref[...]

    @pl.when(head == 0)
    def _():
        k = kv_ref[:, :width].astype(F32)
        k_rot[...] = (k * cosine + pltpu.roll(k, half, 1) * signed).astype(BF)
        dk_sum[...] = jnp.zeros_like(dk_sum)
        dv_sum[...] = jnp.zeros_like(dv_sum)

    values = kv_ref[:, width:]
    keys = k_rot[...]
    q = q_ref[...].astype(F32)
    q_rot = (q * cosine + pltpu.roll(q, half, 1) * signed).astype(BF)
    factor = 1.0 / math.sqrt(width)
    scores = dot(q_rot, keys, ((1,), (1,))) * factor
    visible = pos_row_ref[...] <= pos_col_ref[...]
    scores = jnp.where(visible, scores, -1e30)
    raised = jnp.exp(scores - jnp.max(scores, axis=1, keepdims=True))
    weights = raised / jnp.sum(raised, axis=1, keepdims=True)
    weights_low = weights.astype(BF)
    out_ref[...] = dot(weights_low, values, ((1,), (0,))).astype(BF)
    cotangent = og_ref[...]
    dv_sum[...] += dot(weights_low, cotangent, ((0,), (0,)))
    d_weights = dot(cotangent, values, ((1,), (1,)))
    delta = jnp.sum(d_weights * weights, axis=1, keepdims=True)
    d_scores = (weights * (d_weights - delta) * factor).astype(BF)
    dq = dot(d_scores, keys, ((1,), (0,)))
    dk_sum[...] += dot(d_scores, q_rot, ((0,), (0,)))
    dq_ref[...] = (dq * cosine + pltpu.roll(dq * signed, half, 1)).astype(BF)

    @pl.when(head == heads - 1)
    def _():
        dk = dk_sum[...]
        dkv_ref[:, :width] = (dk * cosine + pltpu.roll(dk * signed, half, 1)).astype(BF)
        dkv_ref[:, width:] = dv_sum[...].astype(BF)


def attention(projected, heads, width, cos_t, sin_t, positions, out_grad):
    length = projected.shape[0]
    q_cols = heads * width
    whole = lambda shape: pl.BlockSpec(shape, lambda h: (0, 0))
    column = pl.BlockSpec((length, width), lambda h: (0, h))
    return pl.pallas_call(
        attention_kernel,
        grid=(heads,),
        in_specs=[
            column,
            pl.BlockSpec((length, 2 * width), lambda h: (0, heads // 2)),
            whole((length, width)),
            whole((length, width)),
            whole((1, length)),
            whole((length, 1)),
            column,
        ],
        out_specs=[column, column, whole((length, 2 * width))],
        out_shape=[
            jax.ShapeDtypeStruct((length, q_cols), BF),
            jax.ShapeDtypeStruct((length, q_cols), BF),
            jax.ShapeDtypeStruct((length, 2 * width), BF),
        ],
        scratch_shapes=[
            pltpu.VMEM((length, width), BF),
            pltpu.VMEM((length, width), F32),
            pltpu.VMEM((length, width), F32),
        ],
        compiler_params=pltpu.CompilerParams(vmem_limit_bytes=24 * 2**20),
        cost_estimate=pl.CostEstimate(
            flops=10 * heads * length * length * width * 2,
            bytes_accessed=6 * length * q_cols * 2,
            transcendentals=heads * length * length,
        ),
    )(projected, projected, cos_t, sin_t, positions[None, :], positions[:, None], out_grad)


def shifted(value, axis, step):
    count = lax.axis_size(axis)
    return lax.ppermute(value, axis, [(i, (i + step) % count) for i in range(count)])


def shifted_chips(value, step):
    count = lax.axis_size("tensor")
    chips = count // 2
    pairs = [(i, ((i // 2 + step) % chips) * 2 + i % 2) for i in range(count)]
    return lax.ppermute(value, "tensor", pairs)


def other_core(value):
    return lax.ppermute(value, "tensor", [(i, i ^ 1) for i in range(lax.axis_size("tensor"))])


def roll_blocks(value, axis, shift, count):
    block = value.shape[axis] // count
    doubled = jnp.concatenate([value, value], axis=axis)
    return lax.dynamic_slice_in_dim(doubled, shift * block, value.shape[axis], axis=axis)


def gather_ring(value):
    after = shifted(value, "dp", -1)
    before = shifted(value, "dp", 1)
    half = value.shape[0] // 2
    far = jnp.concatenate(
        [shifted(before[:half], "dp", 1), shifted(after[half:], "dp", -1)], axis=0
    )
    return [value, after, far, before]


def on_device(act, direction, positions, w_query, w_keyval, out_grad):
    section = lax.axis_index("pipe")
    sections = lax.axis_size("pipe")
    tensor = lax.axis_index("tensor")
    chip, core = tensor // 2, tensor % 2
    chips = lax.axis_size("tensor") // 2
    replica = lax.axis_index("dp")
    replicas = lax.axis_size("dp")
    d_rows, heads, width = w_query.shape[1:]
    seq_len = positions.shape[2]
    q_cols = heads * width
    piece = act.shape[2]

    own_weight = quantize(w_query[0].reshape(d_rows, -1), w_keyval[0].reshape(d_rows, -1))
    weights = gather_ring(own_weight)

    fresh = act[0, 0]
    ends = sections - 1
    from_below = lax.ppermute(fresh, "pipe", [(i, i + 1) for i in range(ends)])
    from_above = lax.ppermute(fresh, "pipe", [(i + 1, i) for i in range(ends)])
    heading = lax.dynamic_index_in_dim(direction, section, 0, keepdims=False)[0]
    down_src = jnp.where(section == 0, fresh, from_below)
    up_src = jnp.where(section == ends, fresh, from_above)
    own = roll_blocks(jnp.where(heading == 0, down_src, up_src), 1, replica, replicas)
    same_core = jnp.concatenate([own] + [shifted_chips(own, -k) for k in range(1, chips)], axis=0)
    tokens = jnp.concatenate([same_core, other_core(same_core)], axis=0)

    def to_relative(value):
        rest = value.shape[1:]
        value = value.reshape((chips, 2, piece) + rest)
        value = roll_blocks(value, 0, chip, chips)
        pair = jnp.where(
            core == 0, jnp.stack([value[:, 0], value[:, 1]]), jnp.stack([value[:, 1], value[:, 0]])
        )
        return pair.reshape((seq_len,) + rest)

    def to_absolute(value):
        rest = value.shape[1:]
        value = value.reshape((2, chips, piece) + rest)
        pair = jnp.where(
            core == 0, jnp.stack([value[0], value[1]], 1), jnp.stack([value[1], value[0]], 1)
        )
        return roll_blocks(pair, 0, (chips - chip) % chips, chips).reshape((seq_len,) + rest)

    pos = to_relative(positions[0, 0][:, None])[:, 0]
    cotangent = to_relative(out_grad[0, 0].reshape(seq_len, -1))
    half = width // 2
    inv_freq = 1000000.0 ** (-jnp.arange(half, dtype=F32) / half)
    angles = pos.astype(F32)[:, None] * inv_freq[None, :]
    cosine, sine = jnp.cos(angles), jnp.sin(angles)
    cos_t = jnp.concatenate([cosine, cosine], axis=1)
    sin_t = jnp.concatenate([-sine, sine], axis=1)

    projected = sum(
        dot(tokens[:, j * d_rows : (j + 1) * d_rows], weights[j], ((1,), (0,)))
        for j in (0, 1, 3, 2)
    ).astype(BF)

    near = seq_len // 2
    sent = [
        shifted(tokens[:near, k * d_rows : (k + 1) * d_rows], "dp", k) for k in range(1, replicas)
    ]
    sent_far = other_core(jnp.stack(sent))
    others = {
        replicas - k: jnp.concatenate([sent[k - 1], sent_far[k - 1]], axis=0)
        for k in range(1, replicas)
    }

    attended, dq, dkv = attention(projected, heads, width, cos_t, sin_t, pos, cotangent)
    attn_out = to_absolute(attended).reshape(1, 1, seq_len, heads, width)

    d_proj = jnp.concatenate([dq, dkv], axis=1)

    def partial(rows):
        return jnp.concatenate(
            [dot(rows, weights[j], ((1,), (1,))).astype(BF) for j in range(replicas)], axis=1
        )

    sibling = other_core(partial(d_proj[near:]))
    mine = partial(d_proj[:near])
    chip_sum = mine.astype(F32) + sibling.astype(F32)
    blocks = chip_sum.reshape(chips, piece, -1)
    arrived = [
        shifted_chips(blocks[k].astype(BF), k).astype(F32) for k in range(1, chips)
    ]
    total = (blocks[0] + sum(arrived)).astype(BF)
    grad_input = roll_blocks(total, 1, (replicas - replica) % replicas, replicas)

    def weight_grad(value):
        grads = gather_ring(value)
        total = dot(tokens[:, :d_rows], grads[0], ((0,), (0,)))
        for j in (1, 3, 2):
            total += dot(others[j], grads[j], ((0,), (0,)))
        own = total.astype(BF)
        far = lax.ppermute(own, "pipe", [(i, ends - i) for i in range(sections)])
        return lax.optimization_barrier(own).astype(F32) + far.astype(F32)

    grad_query = weight_grad(dq).reshape(1, d_rows, heads, width)
    grad_keyval = weight_grad(dkv).reshape(1, d_rows, -1, 2, width)
    return attn_out, grad_input[None, None], grad_query, grad_keyval


def solution(mesh):
    return jax.shard_map(
        on_device,
        mesh=mesh,
        in_specs=(
            P("pipe", "dp", "tensor", None),
            P(None, "dp"),
            P("pipe", "dp", None),
            P("pipe", "dp", "tensor", None),
            P("pipe", "dp", "tensor", None, None),
            P("pipe", "dp", None, "tensor", None),
        ),
        out_specs=(
            P("pipe", "dp", None, "tensor", None),
            P("pipe", "dp", "tensor", None),
            P("pipe", "dp", "tensor", None),
            P("pipe", "dp", "tensor", None, None),
        ),
        check_vma=False,
    )
```

```python
import functools
import math

import jax
import jax.numpy as jnp
from jax import lax
from jax.experimental import pallas as pl
from jax.experimental.pallas import tpu as pltpu
from jax.sharding import PartitionSpec as P

BF = jnp.bfloat16
F32 = jnp.float32
GROUP = 128
LIGHT = pl.CostEstimate(flops=1, bytes_accessed=1, transcendentals=0)
VM = pl.BlockSpec(memory_space=pltpu.VMEM)


def sin_turns(r):
    a = jnp.abs(r)
    m = jnp.minimum(a, 0.5 - a)
    x = (2.0 * math.pi) * m
    y = x * x
    p = -1.0 / 39916800.0
    p = p * y + 1.0 / 362880.0
    p = p * y - 1.0 / 5040.0
    p = p * y + 1.0 / 120.0
    p = p * y - 1.0 / 6.0
    s = x + x * (y * p)
    return jnp.where(r < 0, -s, s)


def quantize_block(w):
    top = jnp.max(jnp.abs(w), axis=0, keepdims=True)
    scale = (top + 1e-06) / 7.0
    t = w * (1.0 / scale)
    wave = sin_turns(t - jnp.round(t))
    return scale * (t - wave * (1.0 / (2.0 * math.pi)))


def quantize_kernel(wq_ref, wkv_ref, out_ref):
    columns = wq_ref.shape[1]
    out_ref[:, :columns] = quantize_block(wq_ref[...].astype(F32)).astype(BF)
    out_ref[:, columns:] = quantize_block(wkv_ref[...].astype(F32)).astype(BF)


def quantize(w_query, w_keyval):
    rows, q_cols = w_query.shape
    kv_cols = w_keyval.shape[1]
    cols = q_cols + kv_cols
    return pl.pallas_call(
        quantize_kernel,
        grid=(rows // GROUP,),
        in_specs=[
            pl.BlockSpec((GROUP, q_cols), lambda i: (i, 0)),
            pl.BlockSpec((GROUP, kv_cols), lambda i: (i, 0)),
        ],
        out_specs=pl.BlockSpec((GROUP, cols), lambda i: (i, 0)),
        out_shape=jax.ShapeDtypeStruct((rows, cols), BF),
        compiler_params=pltpu.CompilerParams(vmem_limit_bytes=16 * 2**20),
        cost_estimate=LIGHT,
    )(w_query, w_keyval)


def dot(a, b, dims):
    return lax.dot_general(a, b, (dims, ((), ())), preferred_element_type=F32)


def whole(shape):
    return pl.BlockSpec(shape, lambda *_: (0,) * len(shape))


def tie_kernel(*refs):
    pass


def tie(*values):
    place = [pl.BlockSpec(memory_space=pl.ANY)] * len(values)
    return pl.pallas_call(
        tie_kernel,
        in_specs=place,
        out_specs=place,
        out_shape=[jax.ShapeDtypeStruct(v.shape, v.dtype) for v in values],
        input_output_aliases={i: i for i in range(len(values))},
        cost_estimate=LIGHT,
    )(*values)


def join_kernel(*refs):
    out_ref, row = refs[-1], 0
    for ref in refs[:-1]:
        out_ref[row : row + ref.shape[0], :] = ref[...]
        row += ref.shape[0]


def join(*parts):
    rows = sum(p.shape[0] for p in parts)
    return pl.pallas_call(
        join_kernel,
        in_specs=[VM] * len(parts),
        out_specs=VM,
        out_shape=jax.ShapeDtypeStruct((rows, parts[0].shape[1]), BF),
        compiler_params=pltpu.CompilerParams(vmem_limit_bytes=16 * 2**20),
        cost_estimate=LIGHT,
    )(*parts)


def halves_kernel(w0_ref, w1_ref, x0_ref, x1_ref, pos_ref, chip_ref, w0_out, w1_out, x0_out, x1_out, pos_out, chip_out):
    w0_out[...] = w0_ref[...]
    w1_out[...] = w1_ref[...]
    x0_out[...] = x0_ref[...]
    x1_out[...] = x1_ref[...]
    pos_out[...] = pos_ref[...]
    chip_out[...] = chip_ref[...]


def first_half(value):
    return pl.BlockSpec((value.shape[0] // 2, value.shape[1]), lambda i: (0, 0))


def second_half(value):
    return pl.BlockSpec((value.shape[0] // 2, value.shape[1]), lambda i: (1, 0))


def half_of(value):
    return jax.ShapeDtypeStruct((value.shape[0] // 2, value.shape[1]), value.dtype)


def halves(w0, w1, x0, x1, pos, chip):
    outs = [half_of(w0), half_of(w1), half_of(x0), half_of(x1)]
    outs += [jax.ShapeDtypeStruct(v.shape, v.dtype) for v in (pos, chip)]
    return pl.pallas_call(
        halves_kernel,
        grid=(1,),
        in_specs=[first_half(w0), second_half(w1), first_half(x0), second_half(x1)]
        + [whole(pos.shape), whole(chip.shape)],
        out_specs=[whole(o.shape) for o in outs],
        out_shape=outs,
        compiler_params=pltpu.CompilerParams(vmem_limit_bytes=16 * 2**20),
        cost_estimate=LIGHT,
    )(w0, w1, x0, x1, pos, chip)


def second_step_kernel(d0_ref, d1_ref, up_ref, down_ref, next_ref, prev_ref, d0_out, d1_out, up_out, down_out):
    d0_out[...] = d0_ref[...]
    d1_out[...] = d1_ref[...]
    up_out[...] = (up_ref[...].astype(F32) + next_ref[...].astype(F32)).astype(BF)
    down_out[...] = (down_ref[...].astype(F32) + prev_ref[...].astype(F32)).astype(BF)


def second_step(d0, d1, up, down, next_top, prev_bot):
    outs = [half_of(d0), half_of(d1), half_of(up), half_of(down)]
    return pl.pallas_call(
        second_step_kernel,
        grid=(1,),
        in_specs=[first_half(d0), second_half(d1), first_half(up), first_half(down)]
        + [whole(next_top.shape), whole(prev_bot.shape)],
        out_specs=[whole(o.shape) for o in outs],
        out_shape=outs,
        compiler_params=pltpu.CompilerParams(vmem_limit_bytes=16 * 2**20),
        cost_estimate=LIGHT,
    )(d0, d1, up, down, next_top, prev_bot)


def input_grad_kernel(shift_ref, kept_ref, up_ref, down_ref, up2_ref, down2_ref, out_ref):
    half = up2_ref.shape[0]
    total = kept_ref[...].astype(F32)
    bottom = total[half:] + up_ref[...].astype(F32) + down2_ref[...].astype(F32)
    top = total[:half] + up2_ref[...].astype(F32) + down_ref[...].astype(F32)
    out_ref[:half, :] = top.astype(BF)
    out_ref[half:, :] = bottom.astype(BF)


def input_grad(replica, replicas, kept, up, down, up2, down2):
    rows, model = kept.shape
    tile = model // replicas
    part = lambda r, k: pl.BlockSpec((r, tile), lambda j, s: (k, j))
    return pl.pallas_call(
        input_grad_kernel,
        grid_spec=pltpu.PrefetchScalarGridSpec(
            num_scalar_prefetch=1,
            grid=(replicas,),
            in_specs=[
                part(rows, 0),
                part(rows // 2, 1),
                part(rows // 2, 1),
                part(rows // 2, 0),
                part(rows // 2, 0),
            ],
            out_specs=pl.BlockSpec((rows, tile), lambda j, s: (0, (j + s[0]) % replicas)),
        ),
        out_shape=jax.ShapeDtypeStruct((rows, model), BF),
        compiler_params=pltpu.CompilerParams(vmem_limit_bytes=16 * 2**20),
        cost_estimate=pl.CostEstimate(
            flops=40 * 10**9, bytes_accessed=160 * 2**20, transcendentals=0
        ),
    )(replica.reshape(1), kept, up, down, up2, down2)


def project_kernel(parts, *refs):
    tokens, weights = refs[:parts], refs[parts:-3]
    out_ref, first_ref, held = refs[-3:]

    @pl.when(pl.program_id(0) == 0)
    def _():
        row = 0
        for ref in tokens:
            held[row : row + ref.shape[0], :] = ref[...]
            row += ref.shape[0]
        first_ref[...] = held[:, : first_ref.shape[1]]

    total, at = None, 0
    for ref in weights:
        term = dot(held[:, at : at + ref.shape[0]], ref[...], ((1,), (0,)))
        total = term if total is None else total + term
        at += ref.shape[0]
    out_ref[...] = total.astype(BF)


def project(tokens, weights, first):
    rows = sum(t.shape[0] for t in tokens)
    model = tokens[0].shape[1]
    cols = weights[0].shape[1]
    tile = 256
    return pl.pallas_call(
        functools.partial(project_kernel, len(tokens)),
        grid=(cols // tile,),
        in_specs=[whole(t.shape) for t in tokens]
        + [pl.BlockSpec((w.shape[0], tile), lambda i: (0, i)) for w in weights],
        out_specs=[pl.BlockSpec((rows, tile), lambda i: (0, i)), whole((rows, first))],
        out_shape=[
            jax.ShapeDtypeStruct((rows, cols), BF),
            jax.ShapeDtypeStruct((rows, first), BF),
        ],
        scratch_shapes=[pltpu.VMEM((rows, model), BF)],
        compiler_params=pltpu.CompilerParams(vmem_limit_bytes=32 * 2**20),
        cost_estimate=LIGHT,
    )(*tokens, *weights)


def pack_kernel(parts, *refs):
    outs = refs[parts + 1 :]
    row = 0
    for ref in refs[:parts]:
        rows, cols = ref.shape[0], outs[0].shape[1]
        for i, out in enumerate(outs):
            out[row : row + rows, :] = ref[:, (i + 1) * cols : (i + 2) * cols]
        row += rows


def pack(tokens, cols, after):
    rows = sum(t.shape[0] for t in tokens)
    count = tokens[0].shape[1] // cols - 1
    return pl.pallas_call(
        functools.partial(pack_kernel, len(tokens)),
        in_specs=[pl.BlockSpec(memory_space=pltpu.VMEM)] * len(tokens)
        + [pl.BlockSpec(memory_space=pl.ANY)],
        out_shape=[jax.ShapeDtypeStruct((rows, cols), BF)] * count,
        compiler_params=pltpu.CompilerParams(vmem_limit_bytes=16 * 2**20),
        cost_estimate=LIGHT,
    )(*tokens, after)


def attention_kernel(
    q_ref, kv_ref, cos_ref, sin_ref, pos_row_ref, pos_col_ref, og_ref,
    out_ref, d_ref, k_rot, dk_sum, dv_sum,
):
    width = cos_ref.shape[1]
    half = width // 2
    head = pl.program_id(0)
    heads = pl.num_programs(0)
    cosine = cos_ref[...]
    signed = sin_ref[...]

    @pl.when(head == 0)
    def _():
        k = kv_ref[:, :width].astype(F32)
        k_rot[...] = (k * cosine + pltpu.roll(k, half, 1) * signed).astype(BF)
        dk_sum[...] = jnp.zeros_like(dk_sum)
        dv_sum[...] = jnp.zeros_like(dv_sum)

    values = kv_ref[:, width:]
    keys = k_rot[...]
    q = q_ref[...].astype(F32)
    q_rot = (q * cosine + pltpu.roll(q, half, 1) * signed).astype(BF)
    factor = 1.0 / math.sqrt(width)
    scores = dot(q_rot, keys, ((1,), (1,))) * factor
    visible = pos_row_ref[...] <= pos_col_ref[...]
    scores = jnp.where(visible, scores, -1e30)
    raised = jnp.exp(scores - jnp.max(scores, axis=1, keepdims=True))
    weights = raised / jnp.sum(raised, axis=1, keepdims=True)
    weights_low = weights.astype(BF)
    out_ref[...] = dot(weights_low, values, ((1,), (0,))).astype(BF)
    cotangent = og_ref[...]
    dv_sum[...] += dot(weights_low, cotangent, ((0,), (0,)))
    d_weights = dot(cotangent, values, ((1,), (1,)))
    delta = jnp.sum(d_weights * weights, axis=1, keepdims=True)
    d_scores = (weights * (d_weights - delta) * factor).astype(BF)
    dq = dot(d_scores, keys, ((1,), (0,)))
    dk_sum[...] += dot(d_scores, q_rot, ((0,), (0,)))
    place = pl.ds(pl.multiple_of(head * width, width), width)
    d_ref[:, place] = (dq * cosine + pltpu.roll(dq * signed, half, 1)).astype(BF)

    @pl.when(head == heads - 1)
    def _():
        dk = dk_sum[...]
        q_cols = d_ref.shape[1] - 2 * width
        dk = (dk * cosine + pltpu.roll(dk * signed, half, 1)).astype(BF)
        d_ref[:, q_cols : q_cols + width] = dk
        d_ref[:, q_cols + width :] = dv_sum[...].astype(BF)


def attention(projected, heads, width, cos_t, sin_t, positions, out_grad):
    length, cols = projected.shape
    q_cols = heads * width
    column = pl.BlockSpec((length, width), lambda h: (0, h))
    return pl.pallas_call(
        attention_kernel,
        grid=(heads,),
        in_specs=[
            column,
            pl.BlockSpec((length, 2 * width), lambda h: (0, heads // 2)),
            whole((length, width)),
            whole((length, width)),
            whole((1, length)),
            whole((length, 1)),
            column,
        ],
        out_specs=[column, whole((length, cols))],
        out_shape=[
            jax.ShapeDtypeStruct((length, q_cols), BF),
            jax.ShapeDtypeStruct((length, cols), BF),
        ],
        scratch_shapes=[
            pltpu.VMEM((length, width), BF),
            pltpu.VMEM((length, width), F32),
            pltpu.VMEM((length, width), F32),
        ],
        compiler_params=pltpu.CompilerParams(vmem_limit_bytes=24 * 2**20),
        cost_estimate=LIGHT,
    )(projected, projected, cos_t, sin_t, positions[None, :], positions[:, None], out_grad)


def partial_kernel(parts, rows, cuts, *refs):
    grads = refs[0][rows[0] : rows[1], :]
    weights, rest = refs[1 : 1 + parts], refs[1 + parts :]
    other = None
    if rows[0] == 0:
        other, rest = rest[0], rest[1:]
    at = 0
    for ref in weights:
        columns = slice(at, at + ref.shape[0])
        total = dot(grads, ref[...], ((1,), (1,)))
        if other is not None:
            total += other[:, columns].astype(F32)
        total = total.astype(BF)
        for out, ranges in zip(rest, cuts):
            row = 0
            for low, high in ranges:
                out[row : row + high - low, columns] = total[low:high]
                row += high - low
        at += ref.shape[0]


def partial(grads, weights, other, cuts):
    near, cols = grads.shape[0] // 2, grads.shape[1]
    model = sum(w.shape[0] for w in weights)
    rows = (near, 2 * near) if other is None else (0, near)
    sizes = [sum(high - low for low, high in ranges) for ranges in cuts]
    return pl.pallas_call(
        functools.partial(partial_kernel, len(weights), rows, cuts),
        out_shape=[jax.ShapeDtypeStruct((p, model), BF) for p in sizes],
        compiler_params=pltpu.CompilerParams(vmem_limit_bytes=24 * 2**20),
        cost_estimate=LIGHT,
    )(grads, *weights, *(() if other is None else (other,)))


def weight_grad_kernel(count, first, *refs):
    tokens, grads, rest = refs[:count], refs[count : 2 * count], refs[2 * count :]
    total = None if first else rest[0][...]
    for x, d in zip(tokens, grads):
        term = dot(x[...], d[...], ((0,), (0,)))
        total = term if total is None else total + term
    if first:
        rest[0][...] = total
    else:
        q_ref, kv_ref = rest[1:]
        q_cols = q_ref.shape[1]
        q_ref[...] = total[:, :q_cols].astype(BF)
        kv_ref[...] = total[:, q_cols:].astype(BF)


def weight_grad(tokens, grads, sums, q_cols):
    count = len(tokens)
    d_rows = tokens[0].shape[1]
    cols = grads[0][0].shape[1]
    tile = 256
    block = lambda width: pl.BlockSpec((tile, width), lambda i: (i, 0))
    in_specs = [pl.BlockSpec((t.shape[0], tile), lambda i: (0, i)) for t in tokens]
    for grad, part in grads:
        if part is None:
            in_specs.append(whole(grad.shape))
        else:
            shape = (grad.shape[0] // 2, cols)
            in_specs.append(pl.BlockSpec(shape, functools.partial(lambda p, i: (p, 0), part)))
    if sums is None:
        operands = ()
        out_specs = block(cols)
        out_shape = jax.ShapeDtypeStruct((d_rows, cols), F32)
    else:
        operands = (sums,)
        in_specs.append(block(cols))
        out_specs = [block(q_cols), block(cols - q_cols)]
        out_shape = [
            jax.ShapeDtypeStruct((d_rows, q_cols), BF),
            jax.ShapeDtypeStruct((d_rows, cols - q_cols), BF),
        ]
    return pl.pallas_call(
        functools.partial(weight_grad_kernel, count, sums is None),
        grid=(d_rows // tile,),
        in_specs=in_specs,
        out_specs=out_specs,
        out_shape=out_shape,
        compiler_params=pltpu.CompilerParams(vmem_limit_bytes=24 * 2**20),
        cost_estimate=LIGHT,
    )(*tokens, *[g for g, _ in grads], *operands)


def mirror_sum_kernel(q_ref, q_far_ref, kv_ref, kv_far_ref, out_q_ref, out_kv_ref):
    width = out_q_ref.shape[-1]
    q = q_ref[...].astype(F32) + q_far_ref[...].astype(F32)
    kv = kv_ref[...].astype(F32) + kv_far_ref[...].astype(F32)
    for i in range(out_q_ref.shape[1]):
        out_q_ref[:, i, :] = q[:, i * width : (i + 1) * width]
    for i in range(out_kv_ref.shape[1]):
        out_kv_ref[:, i, :] = kv[:, i * width : (i + 1) * width]


def mirror_sum(q, q_far, kv, kv_far, width):
    rows, q_cols = q.shape
    kv_cols = kv.shape[1]
    tile = 256
    flat = lambda cols: pl.BlockSpec((tile, cols), lambda i: (i, 0))
    deep = lambda cols: pl.BlockSpec((tile, cols // width, width), lambda i: (i, 0, 0))
    return pl.pallas_call(
        mirror_sum_kernel,
        grid=(rows // tile,),
        in_specs=[flat(q_cols), flat(q_cols), flat(kv_cols), flat(kv_cols)],
        out_specs=[deep(q_cols), deep(kv_cols)],
        out_shape=[
            jax.ShapeDtypeStruct((rows, q_cols // width, width), F32),
            jax.ShapeDtypeStruct((rows, kv_cols // width, width), F32),
        ],
        compiler_params=pltpu.CompilerParams(vmem_limit_bytes=16 * 2**20),
        cost_estimate=LIGHT,
    )(q, q_far, kv, kv_far)


def shifted(value, axis, step):
    count = lax.axis_size(axis)
    return lax.ppermute(value, axis, [(i, (i + step) % count) for i in range(count)])


def shifted_chips(value, step):
    count = lax.axis_size("tensor")
    chips = count // 2
    pairs = [(i, ((i // 2 + step) % chips) * 2 + i % 2) for i in range(count)]
    return lax.ppermute(value, "tensor", pairs)


def other_core(value):
    return lax.ppermute(value, "tensor", [(i, i ^ 1) for i in range(lax.axis_size("tensor"))])


def roll_blocks(value, axis, shift, count):
    block = value.shape[axis] // count
    doubled = jnp.concatenate([value, value], axis=axis)
    return lax.dynamic_slice_in_dim(doubled, shift * block, value.shape[axis], axis=axis)


def on_device(act, direction, positions, w_query, w_keyval, out_grad):
    section = lax.axis_index("pipe")
    sections = lax.axis_size("pipe")
    tensor = lax.axis_index("tensor")
    chip, core = tensor // 2, tensor % 2
    chips = lax.axis_size("tensor") // 2
    replica = lax.axis_index("dp")
    replicas = lax.axis_size("dp")
    d_rows, heads, width = w_query.shape[1:]
    seq_len = positions.shape[2]
    q_cols = heads * width
    piece = act.shape[2]
    near = seq_len // 2
    half = piece // 2

    fresh = act[0, 0]
    ends = sections - 1
    from_below = lax.ppermute(fresh, "pipe", [(i, i + 1) for i in range(ends)])
    from_above = lax.ppermute(fresh, "pipe", [(i + 1, i) for i in range(ends)])

    w_own = quantize(w_query[0].reshape(d_rows, -1), w_keyval[0].reshape(d_rows, -1))
    w_before = shifted(w_own, "dp", 1)
    w_after = shifted(w_own, "dp", -1)

    heading = lax.dynamic_index_in_dim(direction, section, 0, keepdims=False)[0]
    down_src = jnp.where(section == 0, fresh, from_below)
    up_src = jnp.where(section == ends, fresh, from_above)
    own = roll_blocks(jnp.where(heading == 0, down_src, up_src), 1, replica, replicas)
    prev = shifted_chips(own, 1)
    after = shifted_chips(own, -1)

    before_top, after_bot, prev_top, next_bot, late_pos, late_chip = halves(
        w_before, w_after, prev, after, positions[0], chip.reshape(1, 1)
    )
    late_chip = late_chip[0, 0]
    far_top = shifted(before_top, "dp", 1)
    far_bot = shifted(after_bot, "dp", -1)
    across_top = shifted_chips(prev_top, 1)
    across_bot = shifted_chips(next_bot, -1)

    close = join(own, after, prev)
    across = join(across_top, across_bot)
    token_parts = [close, across]
    other_parts = [other_core(part) for part in token_parts]

    def to_relative(value):
        rest = value.shape[1:]
        value = value.reshape((chips, 2, piece) + rest)
        value = roll_blocks(value, 0, late_chip, chips)
        value = jnp.concatenate([value[:2], value[3:], value[2:3]])
        pair = jnp.where(
            core == 0, jnp.stack([value[:, 0], value[:, 1]]), jnp.stack([value[:, 1], value[:, 0]])
        )
        return pair.reshape((seq_len,) + rest)

    def to_absolute(value):
        rest = value.shape[1:]
        value = value.reshape((2, chips, piece) + rest)
        pair = jnp.where(
            core == 0, jnp.stack([value[0], value[1]], 1), jnp.stack([value[1], value[0]], 1)
        )
        pair = jnp.concatenate([pair[:2], pair[3:], pair[2:3]])
        return roll_blocks(pair, 0, (chips - chip) % chips, chips).reshape((seq_len,) + rest)

    pos = to_relative(late_pos[0][:, None])[:, 0]
    cotangent = to_relative(out_grad[0, 0].reshape(seq_len, -1))
    angle_half = width // 2
    inv_freq = 1000000.0 ** (-jnp.arange(angle_half, dtype=F32) / angle_half)
    angles = pos.astype(F32)[:, None] * inv_freq[None, :]
    cosine, sine = jnp.cos(angles), jnp.sin(angles)
    cos_t = jnp.concatenate([cosine, cosine], axis=1)
    sin_t = jnp.concatenate([-sine, sine], axis=1)

    blocks = pack(token_parts, d_rows, far_top)
    sent = [shifted(blocks[k - 1], "dp", k) for k in range(1, replicas)]

    weights = [w_own, w_after, far_top, far_bot, w_before]
    projected, x_own = project(token_parts + other_parts, weights, d_rows)
    attended, d_own = attention(projected, heads, width, cos_t, sin_t, pos, cotangent)
    sent[0], sent[2], d_own = tie(sent[0], sent[2], d_own)
    attn_out = to_absolute(attended).reshape(1, 1, seq_len, heads, width)

    other_part = other_core(partial(d_own, weights, None, [[(0, near)]])[0])
    low = [i * piece for i in range(chips)]
    mid = [i * piece + half for i in range(chips)]
    high = [(i + 1) * piece for i in range(chips)]
    kept, up, next_top, down, prev_bot = partial(
        d_own,
        weights,
        other_part,
        [
            [(low[0], high[0])],
            [(low[3], mid[3]), (mid[1], high[1])],
            [(low[1], mid[1])],
            [(mid[3], high[3]), (low[2], mid[2])],
            [(mid[2], high[2])],
        ],
    )
    up = shifted_chips(up, 1)
    down = shifted_chips(down, -1)

    d_before = shifted(d_own, "dp", 1)
    d_after = shifted(d_own, "dp", -1)
    before_top, after_bot, up2, down2 = second_step(
        d_before, d_after, up, down, next_top, prev_bot
    )
    d_far_top = shifted(before_top, "dp", 1)
    d_far_bot = shifted(after_bot, "dp", -1)
    up2 = shifted_chips(up2, 1)
    down2 = shifted_chips(down2, -1)
    grad_input = input_grad(replica, replicas, kept, up, down, up2, down2)

    near_other = other_core(join(sent[0], sent[2]))
    sums = weight_grad(
        [x_own, sent[0], near_other[:near], sent[2], near_other[near:]],
        [(d_own, None), (d_before, 0), (d_before, 1), (d_after, 0), (d_after, 1)],
        None,
        q_cols,
    )
    own_q, own_kv = weight_grad(
        [sent[1], other_core(sent[1])], [(d_far_top, None), (d_far_bot, None)], sums, q_cols
    )
    pairs = [(i, ends - i) for i in range(sections)]
    far_q = lax.ppermute(own_q, "pipe", pairs)
    far_kv = lax.ppermute(own_kv, "pipe", pairs)
    grad_query, grad_keyval = mirror_sum(own_q, far_q, own_kv, far_kv, width)
    return attn_out, grad_input[None, None], grad_query[None], grad_keyval[None, :, None]


def solution(mesh):
    return jax.shard_map(
        on_device,
        mesh=mesh,
        in_specs=(
            P("pipe", "dp", "tensor", None),
            P(None, "dp"),
            P("pipe", "dp", None),
            P("pipe", "dp", "tensor", None),
            P("pipe", "dp", "tensor", None, None),
            P("pipe", "dp", None, "tensor", None),
        ),
        out_specs=(
            P("pipe", "dp", None, "tensor", None),
            P("pipe", "dp", "tensor", None),
            P("pipe", "dp", "tensor", None),
            P("pipe", "dp", "tensor", None, None),
        ),
        check_vma=False,
    )
```

```python
import functools
import math

import jax
import jax.numpy as jnp
from jax import lax
from jax.experimental import pallas as pl
from jax.experimental.pallas import tpu as pltpu
from jax.sharding import PartitionSpec as P

BF = jnp.bfloat16
F32 = jnp.float32
GROUP = 128
LIGHT = pl.CostEstimate(flops=1, bytes_accessed=1, transcendentals=0)
VM = pl.BlockSpec(memory_space=pltpu.VMEM)


def sin_turns(r):
    a = jnp.abs(r)
    m = jnp.minimum(a, 0.5 - a)
    x = (2.0 * math.pi) * m
    y = x * x
    p = -1.0 / 39916800.0
    p = p * y + 1.0 / 362880.0
    p = p * y - 1.0 / 5040.0
    p = p * y + 1.0 / 120.0
    p = p * y - 1.0 / 6.0
    s = x + x * (y * p)
    return jnp.where(r < 0, -s, s)


def quantize_block(w):
    top = jnp.max(jnp.abs(w), axis=0, keepdims=True)
    scale = (top + 1e-06) / 7.0
    t = w * (1.0 / scale)
    wave = sin_turns(t - jnp.round(t))
    return scale * (t - wave * (1.0 / (2.0 * math.pi)))


def quantize_kernel(wq_ref, wkv_ref, out_ref):
    columns = wq_ref.shape[1]
    out_ref[:, :columns] = quantize_block(wq_ref[...].astype(F32)).astype(BF)
    out_ref[:, columns:] = quantize_block(wkv_ref[...].astype(F32)).astype(BF)


def quantize(w_query, w_keyval):
    rows, q_cols = w_query.shape
    kv_cols = w_keyval.shape[1]
    cols = q_cols + kv_cols
    return pl.pallas_call(
        quantize_kernel,
        grid=(rows // GROUP,),
        in_specs=[
            pl.BlockSpec((GROUP, q_cols), lambda i: (i, 0)),
            pl.BlockSpec((GROUP, kv_cols), lambda i: (i, 0)),
        ],
        out_specs=pl.BlockSpec((GROUP, cols), lambda i: (i, 0)),
        out_shape=jax.ShapeDtypeStruct((rows, cols), BF),
        compiler_params=pltpu.CompilerParams(vmem_limit_bytes=4 * 2**20),
        cost_estimate=LIGHT,
    )(w_query, w_keyval)


def dot(a, b, dims):
    return lax.dot_general(a, b, (dims, ((), ())), preferred_element_type=F32)


def whole(shape):
    return pl.BlockSpec(shape, lambda *_: (0,) * len(shape))


def copy_kernel(moves, count, *refs):
    sems = refs[-1]
    copies = []
    for n, (source, take, target, put) in enumerate(moves):
        copies.append(
            pltpu.make_async_copy(
                refs[source].at[take], refs[count + target].at[put], sems.at[n]
            )
        )
    for copy in copies:
        copy.start()
    for copy in copies:
        copy.wait()


def copied(inputs, specs, after, moves, shapes):
    count = len(inputs) + len(after)
    return pl.pallas_call(
        functools.partial(copy_kernel, moves, count),
        grid=(1,),
        in_specs=specs + [pl.BlockSpec(memory_space=pl.ANY)] * len(after),
        out_specs=[pl.BlockSpec(memory_space=pltpu.HBM)] * len(shapes),
        out_shape=[jax.ShapeDtypeStruct(shape, BF) for shape in shapes],
        scratch_shapes=[pltpu.SemaphoreType.DMA((len(moves),))],
        compiler_params=pltpu.CompilerParams(vmem_limit_bytes=8 * 2**20),
        cost_estimate=LIGHT,
    )(*inputs, *after)


def halves(first, second, after, both):
    rows, cols = first.shape
    half = rows // 2
    top = (slice(0, half), slice(0, cols))
    if both:
        every = (slice(0, rows), slice(0, cols))
        bottom = (slice(half, rows), slice(0, cols))
        specs = [whole(first.shape), whole(second.shape)]
        rest = (slice(rows, 2 * rows), slice(0, cols))
        moves = [(0, top, 0, top), (1, bottom, 1, top), (0, every, 2, every), (1, every, 2, rest)]
        shapes = [(half, cols)] * 2 + [(2 * rows, cols)]
    else:
        specs = [
            pl.BlockSpec((half, cols), lambda i: (0, 0)),
            pl.BlockSpec((half, cols), lambda i: (1, 0)),
        ]
        moves = [(0, top, 0, top), (1, top, 1, top)]
        shapes = [(half, cols)] * 2
    return copied([first, second], specs, after, moves, shapes)


def pack(tokens, cols, joined, after):
    count = tokens[0].shape[1] // cols - 1
    rows = sum(t.shape[0] for t in tokens)
    moves = []
    for block in range(count):
        row = 0
        for n, part in enumerate(tokens):
            size = part.shape[0]
            take = (slice(0, size), slice((block + 1) * cols, (block + 2) * cols))
            moves.append((n, take, block, (slice(row, row + size), slice(0, cols))))
            row += size
    row, model = 0, tokens[0].shape[1]
    for n in range(len(tokens) - joined, len(tokens)):
        size = tokens[n].shape[0]
        every = (slice(0, size), slice(0, model))
        moves.append((n, every, count, (slice(row, row + size), slice(0, model))))
        row += size
    specs = [whole(t.shape) for t in tokens]
    return copied(tokens, specs, after, moves, [(rows, cols)] * count + [(row, model)])


def relay_kernel(place_ref, fresh_ref, below_ref, above_ref, *rest):
    out_ref = rest[-1]
    source = place_ref[1]

    @pl.when(source == 0)
    def _():
        out_ref[...] = fresh_ref[...]

    @pl.when(source == 1)
    def _():
        out_ref[...] = below_ref[...]

    @pl.when(source == 2)
    def _():
        out_ref[...] = above_ref[...]


def relay(place, blocks, fresh, below, above, after):
    rows, model = fresh.shape
    tile = model // blocks
    source = pl.BlockSpec((rows, tile), lambda j, s: (0, (j + s[0]) % blocks))
    return pl.pallas_call(
        relay_kernel,
        grid_spec=pltpu.PrefetchScalarGridSpec(
            num_scalar_prefetch=1,
            grid=(blocks,),
            in_specs=[source] * 3 + [pl.BlockSpec(memory_space=pl.ANY)] * len(after),
            out_specs=pl.BlockSpec((rows, tile), lambda j, s: (0, j)),
        ),
        out_shape=jax.ShapeDtypeStruct((rows, model), BF),
        compiler_params=pltpu.CompilerParams(vmem_limit_bytes=4 * 2**20),
        cost_estimate=LIGHT,
    )(place, fresh, below, above, *after)


def gather_kernel(place_ref, in_ref, out_ref):
    width = in_ref.shape[2]
    for i in range(in_ref.shape[1]):
        out_ref[:, i * width : (i + 1) * width] = in_ref[:, i, :]


def gather_rows(place, value):
    rows, heads, width = value.shape
    count = place.shape[0]
    tile = rows // count
    return pl.pallas_call(
        gather_kernel,
        grid_spec=pltpu.PrefetchScalarGridSpec(
            num_scalar_prefetch=1,
            grid=(count,),
            in_specs=[pl.BlockSpec((tile, heads, width), lambda i, s: (s[i], 0, 0))],
            out_specs=pl.BlockSpec((tile, heads * width), lambda i, s: (i, 0)),
        ),
        out_shape=jax.ShapeDtypeStruct((rows, heads * width), value.dtype),
        compiler_params=pltpu.CompilerParams(vmem_limit_bytes=4 * 2**20),
        cost_estimate=LIGHT,
    )(place, value)


def scatter_kernel(place_ref, in_ref, after_ref, out_ref):
    width = out_ref.shape[2]
    for i in range(out_ref.shape[1]):
        out_ref[:, i, :] = in_ref[:, i * width : (i + 1) * width]


def scatter_rows(place, value, width, after):
    rows, cols = value.shape
    heads = cols // width
    count = place.shape[0]
    tile = rows // count
    return pl.pallas_call(
        scatter_kernel,
        grid_spec=pltpu.PrefetchScalarGridSpec(
            num_scalar_prefetch=1,
            grid=(count,),
            in_specs=[
                pl.BlockSpec((tile, cols), lambda i, s: (i, 0)),
                pl.BlockSpec(memory_space=pl.ANY),
            ],
            out_specs=pl.BlockSpec((tile, heads, width), lambda i, s: (s[i], 0, 0)),
        ),
        out_shape=jax.ShapeDtypeStruct((rows, heads, width), value.dtype),
        compiler_params=pltpu.CompilerParams(vmem_limit_bytes=4 * 2**20),
        cost_estimate=LIGHT,
    )(place, value, after)


def first_half(value):
    return pl.BlockSpec((value.shape[0] // 2, value.shape[1]), lambda i: (0, 0))


def half_of(value):
    return jax.ShapeDtypeStruct((value.shape[0] // 2, value.shape[1]), value.dtype)


def second_step_kernel(up_ref, down_ref, next_ref, prev_ref, up_out, down_out):
    up_out[...] = (up_ref[...].astype(F32) + next_ref[...].astype(F32)).astype(BF)
    down_out[...] = (down_ref[...].astype(F32) + prev_ref[...].astype(F32)).astype(BF)


def second_step(up, down, next_top, prev_bot):
    outs = [half_of(up), half_of(down)]
    return pl.pallas_call(
        second_step_kernel,
        grid=(1,),
        in_specs=[first_half(up), first_half(down)]
        + [whole(next_top.shape), whole(prev_bot.shape)],
        out_specs=[whole(o.shape) for o in outs],
        out_shape=outs,
        compiler_params=pltpu.CompilerParams(vmem_limit_bytes=4 * 2**20),
        cost_estimate=LIGHT,
    )(up, down, next_top, prev_bot)


def input_grad_kernel(shift_ref, kept_ref, up_ref, down_ref, up2_ref, down2_ref, out_ref):
    half = up2_ref.shape[0]
    total = kept_ref[...].astype(F32)
    bottom = total[half:] + up_ref[...].astype(F32) + down2_ref[...].astype(F32)
    top = total[:half] + up2_ref[...].astype(F32) + down_ref[...].astype(F32)
    out_ref[:half, :] = top.astype(BF)
    out_ref[half:, :] = bottom.astype(BF)


def input_grad(replica, replicas, kept, up, down, up2, down2):
    rows, model = kept.shape
    tile = model // replicas
    part = lambda r, k: pl.BlockSpec((r, tile), lambda j, s: (k, j))
    return pl.pallas_call(
        input_grad_kernel,
        grid_spec=pltpu.PrefetchScalarGridSpec(
            num_scalar_prefetch=1,
            grid=(replicas,),
            in_specs=[
                part(rows, 0),
                part(rows // 2, 1),
                part(rows // 2, 1),
                part(rows // 2, 0),
                part(rows // 2, 0),
            ],
            out_specs=pl.BlockSpec((rows, tile), lambda j, s: (0, (j + s[0]) % replicas)),
        ),
        out_shape=jax.ShapeDtypeStruct((rows, model), BF),
        compiler_params=pltpu.CompilerParams(vmem_limit_bytes=4 * 2**20),
        cost_estimate=pl.CostEstimate(
            flops=40 * 10**9, bytes_accessed=160 * 2**20, transcendentals=0
        ),
    )(replica.reshape(1), kept, up, down, up2, down2)


def project_kernel(parts, *refs):
    tokens, weights = refs[:parts], refs[parts:-3]
    out_ref, first_ref, held = refs[-3:]

    @pl.when(pl.program_id(0) == 0)
    def _():
        row = 0
        for ref in tokens:
            held[row : row + ref.shape[0], :] = ref[...]
            row += ref.shape[0]
        first_ref[...] = held[:, : first_ref.shape[1]]

    total, at = None, 0
    for ref in weights:
        term = dot(held[:, at : at + ref.shape[0]], ref[...], ((1,), (0,)))
        total = term if total is None else total + term
        at += ref.shape[0]
    out_ref[...] = total.astype(BF)


def project(tokens, weights, first):
    rows = sum(t.shape[0] for t in tokens)
    model = tokens[0].shape[1]
    cols = weights[0].shape[1]
    tile = 256
    return pl.pallas_call(
        functools.partial(project_kernel, len(tokens)),
        grid=(cols // tile,),
        in_specs=[whole(t.shape) for t in tokens]
        + [pl.BlockSpec((w.shape[0], tile), lambda i: (0, i)) for w in weights],
        out_specs=[pl.BlockSpec((rows, tile), lambda i: (0, i)), whole((rows, first))],
        out_shape=[
            jax.ShapeDtypeStruct((rows, cols), BF),
            jax.ShapeDtypeStruct((rows, first), BF),
        ],
        scratch_shapes=[pltpu.VMEM((rows, model), BF)],
        compiler_params=pltpu.CompilerParams(vmem_limit_bytes=28 * 2**20),
        cost_estimate=LIGHT,
    )(*tokens, *weights)


def attention_kernel(
    q_ref, kv_ref, cos_ref, sin_ref, pos_row_ref, pos_col_ref, og_ref,
    out_ref, d_ref, k_rot, dk_sum, dv_sum,
):
    width = cos_ref.shape[1]
    half = width // 2
    head = pl.program_id(0)
    heads = pl.num_programs(0)
    cosine = cos_ref[...]
    signed = sin_ref[...]

    @pl.when(head == 0)
    def _():
        k = kv_ref[:, :width].astype(F32)
        k_rot[...] = (k * cosine + pltpu.roll(k, half, 1) * signed).astype(BF)
        dk_sum[...] = jnp.zeros_like(dk_sum)
        dv_sum[...] = jnp.zeros_like(dv_sum)

    values = kv_ref[:, width:]
    keys = k_rot[...]
    q = q_ref[...].astype(F32)
    q_rot = (q * cosine + pltpu.roll(q, half, 1) * signed).astype(BF)
    factor = 1.0 / math.sqrt(width)
    scores = dot(q_rot, keys, ((1,), (1,)))
    visible = pos_row_ref[...] <= pos_col_ref[...]
    scores = jnp.where(visible, scores, -1e30)
    raised = jnp.exp2(
        (scores - jnp.max(scores, axis=1, keepdims=True)) * (factor * math.log2(math.e))
    )
    weights = raised * (1.0 / jnp.sum(raised, axis=1, keepdims=True))
    weights_low = weights.astype(BF)
    out_ref[...] = dot(weights_low, values, ((1,), (0,))).astype(BF)
    cotangent = og_ref[...]
    dv_sum[...] += dot(weights_low, cotangent, ((0,), (0,)))
    d_weights = dot(cotangent, values, ((1,), (1,)))
    delta = jnp.sum(d_weights * weights, axis=1, keepdims=True)
    d_scores = (weights * (d_weights - delta)).astype(BF)
    dq = dot(d_scores, keys, ((1,), (0,))) * factor
    dk_sum[...] += dot(d_scores, q_rot, ((0,), (0,)))
    place = pl.ds(pl.multiple_of(head * width, width), width)
    d_ref[:, place] = (dq * cosine + pltpu.roll(dq * signed, half, 1)).astype(BF)

    @pl.when(head == heads - 1)
    def _():
        dk = dk_sum[...] * factor
        q_cols = d_ref.shape[1] - 2 * width
        dk = (dk * cosine + pltpu.roll(dk * signed, half, 1)).astype(BF)
        d_ref[:, q_cols : q_cols + width] = dk
        d_ref[:, q_cols + width :] = dv_sum[...].astype(BF)


def attention(projected, heads, width, cos_t, sin_t, positions, out_grad):
    length, cols = projected.shape
    q_cols = heads * width
    column = pl.BlockSpec((length, width), lambda h: (0, h))
    return pl.pallas_call(
        attention_kernel,
        grid=(heads,),
        in_specs=[
            column,
            pl.BlockSpec((length, 2 * width), lambda h: (0, heads // 2)),
            whole((length, width)),
            whole((length, width)),
            whole((1, length)),
            whole((length, 1)),
            column,
        ],
        out_specs=[column, whole((length, cols))],
        out_shape=[
            jax.ShapeDtypeStruct((length, q_cols), BF),
            jax.ShapeDtypeStruct((length, cols), BF),
        ],
        scratch_shapes=[
            pltpu.VMEM((length, width), BF),
            pltpu.VMEM((length, width), F32),
            pltpu.VMEM((length, width), F32),
        ],
        compiler_params=pltpu.CompilerParams(vmem_limit_bytes=16 * 2**20),
        cost_estimate=LIGHT,
    )(projected, projected, cos_t, sin_t, positions[None, :], positions[:, None], out_grad)


def partial_kernel(parts, rows, *refs):
    weights, (out_ref, held, sems) = refs[1 : 1 + parts], refs[-3:]
    copies, at = [], 0
    for n, ref in enumerate(weights):
        size = ref.shape[0]
        copies.append(pltpu.make_async_copy(ref, held.at[at : at + size, :], sems.at[n]))
        at += size
    for copy in copies:
        copy.start()
    grads = refs[0][rows[0] : rows[1], :]
    at = 0
    for copy, ref in zip(copies, weights):
        columns = slice(at, at + ref.shape[0])
        copy.wait()
        out_ref[:, columns] = dot(grads, held[columns, :], ((1,), (1,))).astype(BF)
        at += ref.shape[0]


def partial(grads, weights, rows, after):
    cols = grads.shape[1]
    model = sum(w.shape[0] for w in weights)
    anywhere = pl.BlockSpec(memory_space=pl.ANY)
    return pl.pallas_call(
        functools.partial(partial_kernel, len(weights), rows),
        in_specs=[VM] + [anywhere] * (len(weights) + len(after)),
        out_specs=VM,
        out_shape=jax.ShapeDtypeStruct((rows[1] - rows[0], model), BF),
        scratch_shapes=[
            pltpu.VMEM((model, cols), BF),
            pltpu.SemaphoreType.DMA((len(weights),)),
        ],
        compiler_params=pltpu.CompilerParams(vmem_limit_bytes=12 * 2**20),
        cost_estimate=LIGHT,
    )(grads, *weights, *after)


def chip_sum_kernel(cuts, a_ref, b_ref, *outs):
    for out, ranges in zip(outs, cuts):
        row = 0
        for low, high in ranges:
            total = a_ref[low:high, :].astype(F32) + b_ref[low:high, :].astype(F32)
            out[row : row + high - low, :] = total.astype(BF)
            row += high - low


def chip_sum(a, b, cuts):
    rows, model = a.shape
    tile = model // 4
    sizes = [sum(high - low for low, high in ranges) for ranges in cuts]
    block = lambda r: pl.BlockSpec((r, tile), lambda j: (0, j))
    return pl.pallas_call(
        functools.partial(chip_sum_kernel, cuts),
        grid=(model // tile,),
        in_specs=[block(rows)] * 2,
        out_specs=[block(size) for size in sizes],
        out_shape=[jax.ShapeDtypeStruct((size, model), BF) for size in sizes],
        compiler_params=pltpu.CompilerParams(vmem_limit_bytes=6 * 2**20),
        cost_estimate=LIGHT,
    )(a, b)


def weight_grad_kernel(count, first, *refs):
    tokens, grads, rest = refs[:count], refs[count : 2 * count], refs[2 * count :]
    rest = rest[-1:] if first else rest[:1] + rest[-2:]
    total = None if first else rest[0][...]
    for x, d in zip(tokens, grads):
        term = dot(x[...], d[...], ((0,), (0,)))
        total = term if total is None else total + term
    if first:
        rest[0][...] = total
    else:
        q_ref, kv_ref = rest[1:]
        q_cols = q_ref.shape[1]
        q_ref[...] = total[:, :q_cols].astype(BF)
        kv_ref[...] = total[:, q_cols:].astype(BF)


def weight_grad(tokens, grads, sums, q_cols, after=()):
    count = len(tokens)
    d_rows = tokens[0].shape[1]
    cols = grads[0][0].shape[1]
    tile = 256
    block = lambda width: pl.BlockSpec((tile, width), lambda i: (i, 0))
    in_specs = [pl.BlockSpec((t.shape[0], tile), lambda i: (0, i)) for t in tokens]
    for grad, part in grads:
        if part is None:
            in_specs.append(whole(grad.shape))
        else:
            shape = (grad.shape[0] // 2, cols)
            in_specs.append(pl.BlockSpec(shape, functools.partial(lambda p, i: (p, 0), part)))
    if sums is None:
        operands = tuple(after)
        in_specs += [pl.BlockSpec(memory_space=pl.ANY)] * len(after)
        out_specs = block(cols)
        out_shape = jax.ShapeDtypeStruct((d_rows, cols), F32)
    else:
        operands = (sums,) + tuple(after)
        in_specs.append(block(cols))
        in_specs += [pl.BlockSpec(memory_space=pl.ANY)] * len(after)
        out_specs = [block(q_cols), block(cols - q_cols)]
        out_shape = [
            jax.ShapeDtypeStruct((d_rows, q_cols), BF),
            jax.ShapeDtypeStruct((d_rows, cols - q_cols), BF),
        ]
    return pl.pallas_call(
        functools.partial(weight_grad_kernel, count, sums is None),
        grid=(d_rows // tile,),
        in_specs=in_specs,
        out_specs=out_specs,
        out_shape=out_shape,
        compiler_params=pltpu.CompilerParams(vmem_limit_bytes=13 * 2**20),
        cost_estimate=LIGHT,
    )(*tokens, *[g for g, _ in grads], *operands)


def mirror_sum_kernel(q_ref, q_far_ref, kv_ref, kv_far_ref, *rest):
    out_q_ref, out_kv_ref = rest[-2:]
    width = out_q_ref.shape[-1]
    q = q_ref[...].astype(F32) + q_far_ref[...].astype(F32)
    kv = kv_ref[...].astype(F32) + kv_far_ref[...].astype(F32)
    for i in range(out_q_ref.shape[1]):
        out_q_ref[:, i, :] = q[:, i * width : (i + 1) * width]
    for i in range(out_kv_ref.shape[1]):
        out_kv_ref[:, i, :] = kv[:, i * width : (i + 1) * width]


def mirror_sum(q, q_far, kv, kv_far, after, width):
    rows, q_cols = q.shape
    kv_cols = kv.shape[1]
    tile = 256
    flat = lambda cols: pl.BlockSpec((tile, cols), lambda i: (i, 0))
    deep = lambda cols: pl.BlockSpec((tile, cols // width, width), lambda i: (i, 0, 0))
    return pl.pallas_call(
        mirror_sum_kernel,
        grid=(rows // tile,),
        in_specs=[flat(q_cols), flat(q_cols), flat(kv_cols), flat(kv_cols)]
        + [pl.BlockSpec(memory_space=pl.ANY)] * len(after),
        out_specs=[deep(q_cols), deep(kv_cols)],
        out_shape=[
            jax.ShapeDtypeStruct((rows, q_cols // width, width), F32),
            jax.ShapeDtypeStruct((rows, kv_cols // width, width), F32),
        ],
        compiler_params=pltpu.CompilerParams(vmem_limit_bytes=6 * 2**20),
        cost_estimate=LIGHT,
    )(q, q_far, kv, kv_far, *after)


def shifted(value, axis, step):
    count = lax.axis_size(axis)
    return lax.ppermute(value, axis, [(i, (i + step) % count) for i in range(count)])


def shifted_chips(value, step):
    count = lax.axis_size("tensor")
    chips = count // 2
    pairs = [(i, ((i // 2 + step) % chips) * 2 + i % 2) for i in range(count)]
    return lax.ppermute(value, "tensor", pairs)


def other_core(value):
    return lax.ppermute(value, "tensor", [(i, i ^ 1) for i in range(lax.axis_size("tensor"))])


def roll_blocks(value, axis, shift, count):
    block = value.shape[axis] // count
    doubled = jnp.concatenate([value, value], axis=axis)
    return lax.dynamic_slice_in_dim(doubled, shift * block, value.shape[axis], axis=axis)


def on_device(act, direction, positions, w_query, w_keyval, out_grad):
    section = lax.axis_index("pipe")
    sections = lax.axis_size("pipe")
    tensor = lax.axis_index("tensor")
    chip, core = tensor // 2, tensor % 2
    chips = lax.axis_size("tensor") // 2
    replica = lax.axis_index("dp")
    replicas = lax.axis_size("dp")
    d_rows, heads, width = w_query.shape[1:]
    seq_len = positions.shape[2]
    q_cols = heads * width
    piece = act.shape[2]
    near = seq_len // 2
    half = piece // 2

    fresh = act[0, 0]
    ends = sections - 1
    from_below = lax.ppermute(fresh, "pipe", [(i, i + 1) for i in range(ends)])
    from_above = lax.ppermute(fresh, "pipe", [(i + 1, i) for i in range(ends)])

    w_own = quantize(w_query[0].reshape(d_rows, -1), w_keyval[0].reshape(d_rows, -1))
    w_before = shifted(w_own, "dp", 1)
    w_after = shifted(w_own, "dp", -1)

    heading = lax.dynamic_index_in_dim(direction, section, 0, keepdims=False)[0]
    source = jnp.where(
        heading == 0, jnp.where(section == 0, 0, 1), jnp.where(section == ends, 0, 2)
    )
    order = jnp.array([0, 1, chips - 1, 2], jnp.int32)
    order = (chip + order) % chips
    place = jnp.concatenate([order * 2 + core, order * 2 + 1 - core])
    pos = jnp.take(positions[0, 0].reshape(-1, piece), place, axis=0).reshape(-1)
    cotangent = gather_rows(place, out_grad[0, 0])
    angle_half = width // 2
    inv_freq = 1000000.0 ** (-jnp.arange(angle_half, dtype=F32) / angle_half)
    angles = pos.astype(F32)[:, None] * inv_freq[None, :]
    cosine, sine = jnp.cos(angles), jnp.sin(angles)
    cos_t = jnp.concatenate([cosine, cosine], axis=1)
    sin_t = jnp.concatenate([-sine, sine], axis=1)
    own = relay(
        jnp.stack([replica, source]),
        replicas,
        fresh,
        from_below,
        from_above,
        [w_own, cos_t, sin_t, cotangent],
    )
    prev = shifted_chips(own, 1)
    after = shifted_chips(own, -1)

    other_own = other_core(own)
    before_top, after_bot = halves(w_before, w_after, [other_own], False)
    next_top, prev_bot, beside = halves(after, prev, [before_top], True)
    far_top = shifted(before_top, "dp", 1)
    far_bot = shifted(after_bot, "dp", -1)
    across_top = shifted_chips(next_top, -1)
    across_bot = shifted_chips(prev_bot, 1)

    *blocks, across = pack(
        [own, beside, across_top, across_bot], d_rows, 2, [far_top, far_bot]
    )
    sent = [shifted(blocks[k - 1], "dp", k) for k in range(1, replicas)]
    token_parts = [own, beside, across]
    other_parts = [other_own, other_core(beside), other_core(across)]

    weights = [w_own, w_after, far_top, far_bot, w_before]
    projected, x_own = project(token_parts + other_parts, weights, d_rows)
    attended, d_own = attention(projected, heads, width, cos_t, sin_t, pos, cotangent)

    other_part = other_core(partial(d_own, weights, (near, seq_len), sent))
    sent_other = [other_core(x) for x in sent]
    own_part = partial(d_own, weights, (0, near), ())
    low = [i * piece for i in range(chips)]
    mid = [i * piece + half for i in range(chips)]
    high = [(i + 1) * piece for i in range(chips)]
    kept, up, next_top, down, prev_bot = chip_sum(
        own_part,
        other_part,
        [
            [(low[0], high[0])],
            [(low[3], mid[3]), (mid[1], high[1])],
            [(low[1], mid[1])],
            [(mid[3], high[3]), (low[2], mid[2])],
            [(mid[2], high[2])],
        ],
    )
    up = shifted_chips(up, 1)
    down = shifted_chips(down, -1)

    up2_part, down2_part = second_step(up, down, next_top, prev_bot)
    up2 = shifted_chips(up2_part, 1)
    down2 = shifted_chips(down2_part, -1)
    grad_input = input_grad(replica, replicas, kept, up, down, up2, down2)

    d_sent = [shifted(d_own, "dp", k) for k in range(1, replicas)]
    attn_out = scatter_rows(place, attended, width, kept)[None, None]
    sums = weight_grad(
        [x_own, sent[0], sent_other[0], sent[2], sent_other[2]],
        [(d_own, None), (d_sent[0], 0), (d_sent[0], 1), (d_sent[2], 0), (d_sent[2], 1)],
        None,
        q_cols,
        [kept, attn_out],
    )
    own_q, own_kv = weight_grad(
        [sent[1], sent_other[1]], [(d_sent[1], 0), (d_sent[1], 1)], sums, q_cols, [up2_part]
    )
    pairs = [(i, ends - i) for i in range(sections)]
    far_q = lax.ppermute(own_q, "pipe", pairs)
    far_kv = lax.ppermute(own_kv, "pipe", pairs)
    grad_query, grad_keyval = mirror_sum(
        own_q, far_q, own_kv, far_kv, [grad_input], width
    )
    return attn_out, grad_input[None, None], grad_query[None], grad_keyval[None, :, None]


def solution(mesh):
    return jax.shard_map(
        on_device,
        mesh=mesh,
        in_specs=(
            P("pipe", "dp", "tensor", None),
            P(None, "dp"),
            P("pipe", "dp", None),
            P("pipe", "dp", "tensor", None),
            P("pipe", "dp", "tensor", None, None),
            P("pipe", "dp", None, "tensor", None),
        ),
        out_specs=(
            P("pipe", "dp", None, "tensor", None),
            P("pipe", "dp", "tensor", None),
            P("pipe", "dp", "tensor", None),
            P("pipe", "dp", "tensor", None, None),
        ),
        check_vma=False,
    )
```

```python
import functools
import math

import jax
import jax.numpy as jnp
from jax import lax
from jax.experimental import pallas as pl
from jax.experimental.pallas import tpu as pltpu
from jax.sharding import PartitionSpec as P

BF = jnp.bfloat16
F32 = jnp.float32
GROUP = 128
TOKEN = jax.ShapeDtypeStruct((8, 128), jnp.float32)
LIGHT = pl.CostEstimate(flops=1, bytes_accessed=1, transcendentals=0)
VM = pl.BlockSpec(memory_space=pltpu.VMEM)


def sin_turns(r):
    a = jnp.abs(r)
    m = jnp.minimum(a, 0.5 - a)
    x = (2.0 * math.pi) * m
    y = x * x
    p = -1.0 / 39916800.0
    p = p * y + 1.0 / 362880.0
    p = p * y - 1.0 / 5040.0
    p = p * y + 1.0 / 120.0
    p = p * y - 1.0 / 6.0
    s = x + x * (y * p)
    return jnp.where(r < 0, -s, s)


def quantize_block(w):
    top = jnp.max(jnp.abs(w), axis=0, keepdims=True)
    scale = (top + 1e-06) / 7.0
    t = w * (1.0 / scale)
    wave = sin_turns(t - jnp.round(t))
    return scale * (t - wave * (1.0 / (2.0 * math.pi)))


def quantize_kernel(wq_ref, wkv_ref, out_ref):
    columns = wq_ref.shape[1]
    out_ref[:, :columns] = quantize_block(wq_ref[...].astype(F32)).astype(BF)
    out_ref[:, columns:] = quantize_block(wkv_ref[...].astype(F32)).astype(BF)


def quantize(w_query, w_keyval):
    rows, q_cols = w_query.shape
    kv_cols = w_keyval.shape[1]
    cols = q_cols + kv_cols
    return pl.pallas_call(
        quantize_kernel,
        grid=(rows // GROUP,),
        in_specs=[
            pl.BlockSpec((GROUP, q_cols), lambda i: (i, 0)),
            pl.BlockSpec((GROUP, kv_cols), lambda i: (i, 0)),
        ],
        out_specs=pl.BlockSpec((GROUP, cols), lambda i: (i, 0)),
        out_shape=jax.ShapeDtypeStruct((rows, cols), BF),
        compiler_params=pltpu.CompilerParams(vmem_limit_bytes=4 * 2**20),
        cost_estimate=LIGHT,
    )(w_query, w_keyval)


def dot(a, b, dims):
    return lax.dot_general(a, b, (dims, ((), ())), preferred_element_type=F32)


def whole(shape):
    return pl.BlockSpec(shape, lambda *_: (0,) * len(shape))


def copy_kernel(moves, count, *refs):
    sems = refs[-1]
    copies = []
    for n, (source, take, target, put) in enumerate(moves):
        copies.append(
            pltpu.make_async_copy(
                refs[source].at[take], refs[count + target].at[put], sems.at[n]
            )
        )
    for copy in copies:
        copy.start()
    for copy in copies:
        copy.wait()


def copied(inputs, specs, after, moves, shapes):
    count = len(inputs) + len(after)
    return pl.pallas_call(
        functools.partial(copy_kernel, moves, count),
        grid=(1,),
        in_specs=specs + [pl.BlockSpec(memory_space=pl.ANY)] * len(after),
        out_specs=[pl.BlockSpec(memory_space=pltpu.HBM)] * len(shapes),
        out_shape=[jax.ShapeDtypeStruct(shape, BF) for shape in shapes],
        scratch_shapes=[pltpu.SemaphoreType.DMA((len(moves),))],
        compiler_params=pltpu.CompilerParams(vmem_limit_bytes=8 * 2**20),
        cost_estimate=LIGHT,
    )(*inputs, *after)


def halves(first, second, after, both):
    rows, cols = first.shape
    half = rows // 2
    top = (slice(0, half), slice(0, cols))
    if both:
        every = (slice(0, rows), slice(0, cols))
        bottom = (slice(half, rows), slice(0, cols))
        specs = [whole(first.shape), whole(second.shape)]
        rest = (slice(rows, 2 * rows), slice(0, cols))
        moves = [(0, top, 0, top), (1, bottom, 1, top), (0, every, 2, every), (1, every, 2, rest)]
        shapes = [(half, cols)] * 2 + [(2 * rows, cols)]
    else:
        specs = [
            pl.BlockSpec((half, cols), lambda i: (0, 0)),
            pl.BlockSpec((half, cols), lambda i: (1, 0)),
        ]
        moves = [(0, top, 0, top), (1, top, 1, top)]
        shapes = [(half, cols)] * 2
    return copied([first, second], specs, after, moves, shapes)


def pack_near(tokens, cols, rows):
    count = tokens[0].shape[1] // cols - 1
    moves = []
    for block in range(count):
        row = 0
        for n, part in enumerate(tokens):
            size = part.shape[0]
            take = (slice(0, size), slice((block + 1) * cols, (block + 2) * cols))
            moves.append((n, take, block, (slice(row, row + size), slice(0, cols))))
            row += size
    specs = [whole(t.shape) for t in tokens]
    return copied(tokens, specs, [], moves, [(rows, cols)] * count)


def pack_kernel(moves, parts, blocks, *refs):
    tokens, outs, sems = refs[:parts], refs[-2 - blocks : -1], refs[-1]
    copies = []
    for n, (source, take, target, put) in enumerate(moves):
        copies.append(
            pltpu.make_async_copy(tokens[source].at[take], outs[target].at[put], sems.at[n])
        )
    for copy in copies:
        copy.start()
    for copy in copies:
        copy.wait()


def pack_rest(tokens, blocks, after):
    rows, cols = blocks[0].shape
    count = len(blocks)
    model = tokens[0].shape[1]
    total = sum(t.shape[0] for t in tokens)
    moves, row = [], 0
    for n, part in enumerate(tokens):
        size = part.shape[0]
        for block in range(count):
            take = (slice(0, size), slice((block + 1) * cols, (block + 2) * cols))
            put = (slice(rows - total + row, rows - total + row + size), slice(0, cols))
            moves.append((n, take, block, put))
        every = (slice(0, size), slice(0, model))
        moves.append((n, every, count, (slice(row, row + size), slice(0, model))))
        row += size
    anywhere = pl.BlockSpec(memory_space=pl.ANY)
    return pl.pallas_call(
        functools.partial(pack_kernel, moves, len(tokens), count),
        grid=(1,),
        in_specs=[whole(t.shape) for t in tokens] + [anywhere] * (count + len(after)),
        out_specs=[anywhere] * (count + 1),
        out_shape=[jax.ShapeDtypeStruct((rows, cols), BF)] * count
        + [jax.ShapeDtypeStruct((total, model), BF)],
        input_output_aliases={len(tokens) + i: i for i in range(count)},
        scratch_shapes=[pltpu.SemaphoreType.DMA((len(moves),))],
        compiler_params=pltpu.CompilerParams(vmem_limit_bytes=8 * 2**20),
        cost_estimate=LIGHT,
    )(*tokens, *blocks, *after)


def relay_kernel(place_ref, fresh_ref, below_ref, above_ref, *rest):
    out_ref = rest[-1]
    source = place_ref[1]

    @pl.when(source == 0)
    def _():
        out_ref[...] = fresh_ref[...]

    @pl.when(source == 1)
    def _():
        out_ref[...] = below_ref[...]

    @pl.when(source == 2)
    def _():
        out_ref[...] = above_ref[...]


def relay(place, blocks, fresh, below, above, after):
    rows, model = fresh.shape
    tile = model // blocks
    source = pl.BlockSpec((rows, tile), lambda j, s: (0, (j + s[0]) % blocks))
    return pl.pallas_call(
        relay_kernel,
        grid_spec=pltpu.PrefetchScalarGridSpec(
            num_scalar_prefetch=1,
            grid=(blocks,),
            in_specs=[source] * 3 + [pl.BlockSpec(memory_space=pl.ANY)] * len(after),
            out_specs=pl.BlockSpec((rows, tile), lambda j, s: (0, j)),
        ),
        out_shape=jax.ShapeDtypeStruct((rows, model), BF),
        compiler_params=pltpu.CompilerParams(vmem_limit_bytes=4 * 2**20),
        cost_estimate=LIGHT,
    )(place, fresh, below, above, *after)


def gather_kernel(place_ref, in_ref, out_ref, token_ref):
    token_ref[...] = jnp.zeros_like(token_ref)
    width = in_ref.shape[2]
    for i in range(in_ref.shape[1]):
        out_ref[:, i * width : (i + 1) * width] = in_ref[:, i, :]


def gather_rows(place, value):
    rows, heads, width = value.shape
    count = place.shape[0]
    tile = rows // count
    return pl.pallas_call(
        gather_kernel,
        grid_spec=pltpu.PrefetchScalarGridSpec(
            num_scalar_prefetch=1,
            grid=(count,),
            in_specs=[pl.BlockSpec((tile, heads, width), lambda i, s: (s[i], 0, 0))],
            out_specs=[
                pl.BlockSpec((tile, heads * width), lambda i, s: (i, 0)),
                whole(TOKEN.shape),
            ],
        ),
        out_shape=[jax.ShapeDtypeStruct((rows, heads * width), value.dtype), TOKEN],
        compiler_params=pltpu.CompilerParams(vmem_limit_bytes=4 * 2**20),
        cost_estimate=LIGHT,
    )(place, value)


def scatter_kernel(place_ref, in_ref, after_ref, out_ref, token_ref):
    token_ref[...] = jnp.zeros_like(token_ref)
    width = out_ref.shape[2]
    for i in range(out_ref.shape[1]):
        out_ref[:, i, :] = in_ref[:, i * width : (i + 1) * width]


def scatter_rows(place, value, width, after):
    rows, cols = value.shape
    heads = cols // width
    count = place.shape[0]
    tile = rows // count
    return pl.pallas_call(
        scatter_kernel,
        grid_spec=pltpu.PrefetchScalarGridSpec(
            num_scalar_prefetch=1,
            grid=(count,),
            in_specs=[
                pl.BlockSpec((tile, cols), lambda i, s: (i, 0)),
                pl.BlockSpec(memory_space=pl.ANY),
            ],
            out_specs=[
                pl.BlockSpec((tile, heads, width), lambda i, s: (s[i], 0, 0)),
                whole(TOKEN.shape),
            ],
        ),
        out_shape=[jax.ShapeDtypeStruct((rows, heads, width), value.dtype), TOKEN],
        compiler_params=pltpu.CompilerParams(vmem_limit_bytes=4 * 2**20),
        cost_estimate=LIGHT,
    )(place, value, after)


def first_half(value):
    return pl.BlockSpec((value.shape[0] // 2, value.shape[1]), lambda i: (0, 0))


def half_of(value):
    return jax.ShapeDtypeStruct((value.shape[0] // 2, value.shape[1]), value.dtype)


def second_step_kernel(up_ref, down_ref, next_ref, prev_ref, *rest):
    up_out, down_out, token_ref = rest[-3:]
    token_ref[...] = jnp.zeros_like(token_ref)
    up_out[...] = (up_ref[...].astype(F32) + next_ref[...].astype(F32)).astype(BF)
    down_out[...] = (down_ref[...].astype(F32) + prev_ref[...].astype(F32)).astype(BF)


def second_step(up, down, next_top, prev_bot, after):
    outs = [half_of(up), half_of(down), TOKEN]
    return pl.pallas_call(
        second_step_kernel,
        grid=(1,),
        in_specs=[first_half(up), first_half(down)]
        + [whole(next_top.shape), whole(prev_bot.shape)]
        + [pl.BlockSpec(memory_space=pl.ANY)] * len(after),
        out_specs=[whole(o.shape) for o in outs],
        out_shape=outs,
        compiler_params=pltpu.CompilerParams(vmem_limit_bytes=4 * 2**20),
        cost_estimate=pl.CostEstimate(
            flops=8 * 10**9, bytes_accessed=1, transcendentals=0
        ),
    )(up, down, next_top, prev_bot, *after)


def input_grad_kernel(
    shift_ref, kept_ref, up_ref, down_ref, up2_ref, down2_ref, out_ref, token_ref
):
    token_ref[...] = jnp.zeros_like(token_ref)
    half = up2_ref.shape[0]
    total = kept_ref[...].astype(F32)
    bottom = total[half:] + up_ref[...].astype(F32) + down2_ref[...].astype(F32)
    top = total[:half] + up2_ref[...].astype(F32) + down_ref[...].astype(F32)
    out_ref[:half, :] = top.astype(BF)
    out_ref[half:, :] = bottom.astype(BF)


def input_grad(replica, replicas, kept, up, down, up2, down2):
    rows, model = kept.shape
    tile = model // replicas
    part = lambda r, k: pl.BlockSpec((r, tile), lambda j, s: (k, j))
    return pl.pallas_call(
        input_grad_kernel,
        grid_spec=pltpu.PrefetchScalarGridSpec(
            num_scalar_prefetch=1,
            grid=(replicas,),
            in_specs=[
                part(rows, 0),
                part(rows // 2, 1),
                part(rows // 2, 1),
                part(rows // 2, 0),
                part(rows // 2, 0),
            ],
            out_specs=[
                pl.BlockSpec((rows, tile), lambda j, s: (0, (j + s[0]) % replicas)),
                whole(TOKEN.shape),
            ],
        ),
        out_shape=[jax.ShapeDtypeStruct((rows, model), BF), TOKEN],
        compiler_params=pltpu.CompilerParams(vmem_limit_bytes=4 * 2**20),
        cost_estimate=pl.CostEstimate(
            flops=40 * 10**9, bytes_accessed=160 * 2**20, transcendentals=0
        ),
    )(replica.reshape(1), kept, up, down, up2, down2)


def project_kernel(parts, *refs):
    tokens, weights = refs[:parts], refs[parts:-3]
    out_ref, first_ref, held = refs[-3:]

    @pl.when(pl.program_id(0) == 0)
    def _():
        row = 0
        for ref in tokens:
            held[row : row + ref.shape[0], :] = ref[...]
            row += ref.shape[0]
        first_ref[...] = held[:, : first_ref.shape[1]]

    total, at = None, 0
    for ref in weights:
        term = dot(held[:, at : at + ref.shape[0]], ref[...], ((1,), (0,)))
        total = term if total is None else total + term
        at += ref.shape[0]
    out_ref[...] = total.astype(BF)


def project(tokens, weights, first):
    rows = sum(t.shape[0] for t in tokens)
    model = tokens[0].shape[1]
    cols = weights[0].shape[1]
    tile = 256
    return pl.pallas_call(
        functools.partial(project_kernel, len(tokens)),
        grid=(cols // tile,),
        in_specs=[whole(t.shape) for t in tokens]
        + [pl.BlockSpec((w.shape[0], tile), lambda i: (0, i)) for w in weights],
        out_specs=[pl.BlockSpec((rows, tile), lambda i: (0, i)), whole((rows, first))],
        out_shape=[
            jax.ShapeDtypeStruct((rows, cols), BF),
            jax.ShapeDtypeStruct((rows, first), BF),
        ],
        scratch_shapes=[pltpu.VMEM((rows, model), BF)],
        compiler_params=pltpu.CompilerParams(vmem_limit_bytes=28 * 2**20),
        cost_estimate=LIGHT,
    )(*tokens, *weights)


def attention_kernel(
    q_ref, kv_ref, cos_ref, sin_ref, pos_row_ref, pos_col_ref, og_ref,
    out_ref, d_ref, k_rot, dk_sum, dv_sum,
):
    width = cos_ref.shape[1]
    half = width // 2
    head = pl.program_id(0)
    heads = pl.num_programs(0)
    cosine = cos_ref[...]
    signed = sin_ref[...]

    @pl.when(head == 0)
    def _():
        k = kv_ref[:, :width].astype(F32)
        k_rot[...] = (k * cosine + pltpu.roll(k, half, 1) * signed).astype(BF)
        dk_sum[...] = jnp.zeros_like(dk_sum)
        dv_sum[...] = jnp.zeros_like(dv_sum)

    values = kv_ref[:, width:]
    keys = k_rot[...]
    q = q_ref[...].astype(F32)
    q_rot = (q * cosine + pltpu.roll(q, half, 1) * signed).astype(BF)
    factor = 1.0 / math.sqrt(width)
    scores = dot(q_rot, keys, ((1,), (1,)))
    visible = pos_row_ref[...] <= pos_col_ref[...]
    scores = jnp.where(visible, scores, -1e30)
    raised = jnp.exp2(
        (scores - jnp.max(scores, axis=1, keepdims=True)) * (factor * math.log2(math.e))
    )
    weights = raised * (1.0 / jnp.sum(raised, axis=1, keepdims=True))
    weights_low = weights.astype(BF)
    out_ref[...] = dot(weights_low, values, ((1,), (0,))).astype(BF)
    cotangent = og_ref[...]
    dv_sum[...] += dot(weights_low, cotangent, ((0,), (0,)))
    d_weights = dot(cotangent, values, ((1,), (1,)))
    delta = jnp.sum(d_weights * weights, axis=1, keepdims=True)
    d_scores = (weights * (d_weights - delta)).astype(BF)
    dq = dot(d_scores, keys, ((1,), (0,))) * factor
    dk_sum[...] += dot(d_scores, q_rot, ((0,), (0,)))
    place = pl.ds(pl.multiple_of(head * width, width), width)
    d_ref[:, place] = (dq * cosine + pltpu.roll(dq * signed, half, 1)).astype(BF)

    @pl.when(head == heads - 1)
    def _():
        dk = dk_sum[...] * factor
        q_cols = d_ref.shape[1] - 2 * width
        dk = (dk * cosine + pltpu.roll(dk * signed, half, 1)).astype(BF)
        d_ref[:, q_cols : q_cols + width] = dk
        d_ref[:, q_cols + width :] = dv_sum[...].astype(BF)


def attention(projected, heads, width, cos_t, sin_t, positions, out_grad):
    length, cols = projected.shape
    q_cols = heads * width
    column = pl.BlockSpec((length, width), lambda h: (0, h))
    return pl.pallas_call(
        attention_kernel,
        grid=(heads,),
        in_specs=[
            column,
            pl.BlockSpec((length, 2 * width), lambda h: (0, heads // 2)),
            whole((length, width)),
            whole((length, width)),
            whole((1, length)),
            whole((length, 1)),
            column,
        ],
        out_specs=[column, whole((length, cols))],
        out_shape=[
            jax.ShapeDtypeStruct((length, q_cols), BF),
            jax.ShapeDtypeStruct((length, cols), BF),
        ],
        scratch_shapes=[
            pltpu.VMEM((length, width), BF),
            pltpu.VMEM((length, width), F32),
            pltpu.VMEM((length, width), F32),
        ],
        compiler_params=pltpu.CompilerParams(vmem_limit_bytes=16 * 2**20),
        cost_estimate=LIGHT,
    )(projected, projected, cos_t, sin_t, positions[None, :], positions[:, None], out_grad)


def partial_kernel(parts, rows, *refs):
    weights, (out_ref, held, sems) = refs[1 : 1 + parts], refs[-3:]
    copies, at = [], 0
    for n, ref in enumerate(weights):
        size = ref.shape[0]
        copies.append(pltpu.make_async_copy(ref, held.at[at : at + size, :], sems.at[n]))
        at += size
    for copy in copies:
        copy.start()
    grads = refs[0][rows[0] : rows[1], :]
    at = 0
    for copy, ref in zip(copies, weights):
        columns = slice(at, at + ref.shape[0])
        copy.wait()
        out_ref[:, columns] = dot(grads, held[columns, :], ((1,), (1,))).astype(BF)
        at += ref.shape[0]


def partial(grads, weights, rows, after):
    cols = grads.shape[1]
    model = sum(w.shape[0] for w in weights)
    anywhere = pl.BlockSpec(memory_space=pl.ANY)
    return pl.pallas_call(
        functools.partial(partial_kernel, len(weights), rows),
        in_specs=[VM] + [anywhere] * (len(weights) + len(after)),
        out_specs=VM,
        out_shape=jax.ShapeDtypeStruct((rows[1] - rows[0], model), BF),
        scratch_shapes=[
            pltpu.VMEM((model, cols), BF),
            pltpu.SemaphoreType.DMA((len(weights),)),
        ],
        compiler_params=pltpu.CompilerParams(vmem_limit_bytes=12 * 2**20),
        cost_estimate=LIGHT,
    )(grads, *weights, *after)


def chip_sum_kernel(cuts, a_ref, b_ref, *rest):
    outs = rest[-1 - len(cuts) : -1]
    rest[-1][...] = jnp.zeros_like(rest[-1])
    for out, ranges in zip(outs, cuts):
        row = 0
        for low, high in ranges:
            total = a_ref[low:high, :].astype(F32) + b_ref[low:high, :].astype(F32)
            out[row : row + high - low, :] = total.astype(BF)
            row += high - low


def chip_sum(a, b, cuts, after):
    rows, model = a.shape
    tile = model // 4
    sizes = [sum(high - low for low, high in ranges) for ranges in cuts]
    block = lambda r: pl.BlockSpec((r, tile), lambda j: (0, j))
    return pl.pallas_call(
        functools.partial(chip_sum_kernel, cuts),
        grid=(model // tile,),
        in_specs=[block(rows)] * 2 + [pl.BlockSpec(memory_space=pl.ANY)] * len(after),
        out_specs=[block(size) for size in sizes] + [whole(TOKEN.shape)],
        out_shape=[jax.ShapeDtypeStruct((size, model), BF) for size in sizes] + [TOKEN],
        compiler_params=pltpu.CompilerParams(vmem_limit_bytes=6 * 2**20),
        cost_estimate=LIGHT,
    )(a, b, *after)


def weight_grad_kernel(count, first, *refs):
    tokens, grads, rest = refs[:count], refs[count : 2 * count], refs[2 * count :]
    rest = rest[-2:] if first else rest[:1] + rest[-2:]
    total = None if first else rest[0][...]
    for x, d in zip(tokens, grads):
        term = dot(x[...], d[...], ((0,), (0,)))
        total = term if total is None else total + term
    if first:
        rest[0][...] = total
        rest[1][...] = jnp.zeros_like(rest[1])
    else:
        q_ref, kv_ref = rest[1:]
        q_cols = q_ref.shape[1]
        q_ref[...] = total[:, :q_cols].astype(BF)
        kv_ref[...] = total[:, q_cols:].astype(BF)


def weight_grad(tokens, grads, sums, q_cols, after=()):
    count = len(tokens)
    d_rows = tokens[0].shape[1]
    cols = grads[0][0].shape[1]
    tile = 256
    block = lambda width: pl.BlockSpec((tile, width), lambda i: (i, 0))
    in_specs = [pl.BlockSpec((t.shape[0], tile), lambda i: (0, i)) for t in tokens]
    for grad, part in grads:
        if part is None:
            in_specs.append(whole(grad.shape))
        else:
            shape = (grad.shape[0] // 2, cols)
            in_specs.append(pl.BlockSpec(shape, functools.partial(lambda p, i: (p, 0), part)))
    if sums is None:
        operands = tuple(after)
        in_specs += [pl.BlockSpec(memory_space=pl.ANY)] * len(after)
        out_specs = [block(cols), whole(TOKEN.shape)]
        out_shape = [jax.ShapeDtypeStruct((d_rows, cols), F32), TOKEN]
    else:
        operands = (sums,) + tuple(after)
        in_specs.append(block(cols))
        in_specs += [pl.BlockSpec(memory_space=pl.ANY)] * len(after)
        out_specs = [block(q_cols), block(cols - q_cols)]
        out_shape = [
            jax.ShapeDtypeStruct((d_rows, q_cols), BF),
            jax.ShapeDtypeStruct((d_rows, cols - q_cols), BF),
        ]
    return pl.pallas_call(
        functools.partial(weight_grad_kernel, count, sums is None),
        grid=(d_rows // tile,),
        in_specs=in_specs,
        out_specs=out_specs,
        out_shape=out_shape,
        compiler_params=pltpu.CompilerParams(vmem_limit_bytes=13 * 2**20),
        cost_estimate=LIGHT,
    )(*tokens, *[g for g, _ in grads], *operands)


def mirror_sum_kernel(q_ref, q_far_ref, kv_ref, kv_far_ref, *rest):
    out_q_ref, out_kv_ref = rest[-2:]
    width = out_q_ref.shape[-1]
    q = q_ref[...].astype(F32) + q_far_ref[...].astype(F32)
    kv = kv_ref[...].astype(F32) + kv_far_ref[...].astype(F32)
    for i in range(out_q_ref.shape[1]):
        out_q_ref[:, i, :] = q[:, i * width : (i + 1) * width]
    for i in range(out_kv_ref.shape[1]):
        out_kv_ref[:, i, :] = kv[:, i * width : (i + 1) * width]


def mirror_sum(q, q_far, kv, kv_far, after, width):
    rows, q_cols = q.shape
    kv_cols = kv.shape[1]
    tile = 256
    flat = lambda cols: pl.BlockSpec((tile, cols), lambda i: (i, 0))
    deep = lambda cols: pl.BlockSpec((tile, cols // width, width), lambda i: (i, 0, 0))
    return pl.pallas_call(
        mirror_sum_kernel,
        grid=(rows // tile,),
        in_specs=[flat(q_cols), flat(q_cols), flat(kv_cols), flat(kv_cols)]
        + [pl.BlockSpec(memory_space=pl.ANY)] * len(after),
        out_specs=[deep(q_cols), deep(kv_cols)],
        out_shape=[
            jax.ShapeDtypeStruct((rows, q_cols // width, width), F32),
            jax.ShapeDtypeStruct((rows, kv_cols // width, width), F32),
        ],
        compiler_params=pltpu.CompilerParams(vmem_limit_bytes=6 * 2**20),
        cost_estimate=LIGHT,
    )(q, q_far, kv, kv_far, *after)


def shifted(value, axis, step):
    count = lax.axis_size(axis)
    return lax.ppermute(value, axis, [(i, (i + step) % count) for i in range(count)])


def shifted_chips(value, step):
    count = lax.axis_size("tensor")
    chips = count // 2
    pairs = [(i, ((i // 2 + step) % chips) * 2 + i % 2) for i in range(count)]
    return lax.ppermute(value, "tensor", pairs)


def other_core(value):
    return lax.ppermute(value, "tensor", [(i, i ^ 1) for i in range(lax.axis_size("tensor"))])


def roll_blocks(value, axis, shift, count):
    block = value.shape[axis] // count
    doubled = jnp.concatenate([value, value], axis=axis)
    return lax.dynamic_slice_in_dim(doubled, shift * block, value.shape[axis], axis=axis)


def on_device(act, direction, positions, w_query, w_keyval, out_grad):
    section = lax.axis_index("pipe")
    sections = lax.axis_size("pipe")
    tensor = lax.axis_index("tensor")
    chip, core = tensor // 2, tensor % 2
    chips = lax.axis_size("tensor") // 2
    replica = lax.axis_index("dp")
    replicas = lax.axis_size("dp")
    d_rows, heads, width = w_query.shape[1:]
    seq_len = positions.shape[2]
    q_cols = heads * width
    piece = act.shape[2]
    near = seq_len // 2
    half = piece // 2

    fresh = act[0, 0]
    ends = sections - 1
    from_below = lax.ppermute(fresh, "pipe", [(i, i + 1) for i in range(ends)])
    from_above = lax.ppermute(fresh, "pipe", [(i + 1, i) for i in range(ends)])

    w_own = quantize(w_query[0].reshape(d_rows, -1), w_keyval[0].reshape(d_rows, -1))
    w_before = shifted(w_own, "dp", 1)
    w_after = shifted(w_own, "dp", -1)

    heading = lax.dynamic_index_in_dim(direction, section, 0, keepdims=False)[0]
    source = jnp.where(
        heading == 0, jnp.where(section == 0, 0, 1), jnp.where(section == ends, 0, 2)
    )
    order = jnp.array([0, 1, chips - 1, 2], jnp.int32)
    order = (chip + order) % chips
    place = jnp.concatenate([order * 2 + core, order * 2 + 1 - core])
    pos = jnp.take(positions[0, 0].reshape(-1, piece), place, axis=0).reshape(-1)
    cotangent, rows_set = gather_rows(place, out_grad[0, 0])
    angle_half = width // 2
    inv_freq = 1000000.0 ** (-jnp.arange(angle_half, dtype=F32) / angle_half)
    angles = pos.astype(F32)[:, None] * inv_freq[None, :]
    cosine, sine = jnp.cos(angles), jnp.sin(angles)
    cos_t = jnp.concatenate([cosine, cosine], axis=1)
    sin_t = jnp.concatenate([-sine, sine], axis=1)
    own = relay(
        jnp.stack([replica, source]),
        replicas,
        fresh,
        from_below,
        from_above,
        [w_own, cos_t, sin_t, rows_set],
    )
    prev = shifted_chips(own, 1)
    after = shifted_chips(own, -1)

    other_own = other_core(own)
    before_top, after_bot = halves(w_before, w_after, [other_own], False)
    next_top, prev_bot, beside = halves(after, prev, [before_top], True)
    far_top = shifted(before_top, "dp", 1)
    far_bot = shifted(after_bot, "dp", -1)
    across_top = shifted_chips(next_top, -1)
    across_bot = shifted_chips(prev_bot, 1)

    blocks = pack_near([own, beside], d_rows, near)
    *blocks, across = pack_rest([across_top, across_bot], blocks, [far_top, far_bot])
    sent = [shifted(blocks[k - 1], "dp", k) for k in range(1, replicas)]
    token_parts = [own, beside, across]
    other_parts = [other_own, other_core(beside), other_core(across)]

    weights = [w_own, w_after, far_top, far_bot, w_before]
    projected, x_own = project(token_parts + other_parts, weights, d_rows)
    attended, d_own = attention(projected, heads, width, cos_t, sin_t, pos, cotangent)

    other_part = other_core(partial(d_own, weights, (near, seq_len), sent))
    sent_other = [other_core(x) for x in sent]
    own_part = partial(d_own, weights, (0, near), ())
    low = [i * piece for i in range(chips)]
    mid = [i * piece + half for i in range(chips)]
    high = [(i + 1) * piece for i in range(chips)]
    kept, up, next_top, down, prev_bot, chip_set = chip_sum(
        own_part,
        other_part,
        [
            [(low[0], high[0])],
            [(low[3], mid[3]), (mid[1], high[1])],
            [(low[1], mid[1])],
            [(mid[3], high[3]), (low[2], mid[2])],
            [(mid[2], high[2])],
        ],
        [],
    )
    up = shifted_chips(up, 1)
    down = shifted_chips(down, -1)

    d_before = shifted(d_own, "dp", 1)
    d_after = shifted(d_own, "dp", -1)
    before_top, after_bot = halves(
        d_before, d_after, [chip_set] + sent_other, False
    )
    d_far_top = shifted(before_top, "dp", 1)
    d_far_bot = shifted(after_bot, "dp", -1)
    attn_out, out_set = scatter_rows(place, attended, width, chip_set)
    attn_out = attn_out[None, None]
    sums, sums_set = weight_grad(
        [x_own, sent[0], sent_other[0], sent[2], sent_other[2]],
        [(d_own, None), (d_before, 0), (d_before, 1), (d_after, 0), (d_after, 1)],
        None,
        q_cols,
        [chip_set, out_set],
    )
    up2_part, down2_part, step_set = second_step(
        up, down, next_top, prev_bot, [sums_set, out_set]
    )
    up2 = shifted_chips(up2_part, 1)
    down2 = shifted_chips(down2_part, -1)
    grad_input, input_set = input_grad(replica, replicas, kept, up, down, up2, down2)
    own_q, own_kv = weight_grad(
        [sent[1], sent_other[1]], [(d_far_top, None), (d_far_bot, None)], sums, q_cols, [step_set]
    )
    pairs = [(i, ends - i) for i in range(sections)]
    far_q = lax.ppermute(own_q, "pipe", pairs)
    far_kv = lax.ppermute(own_kv, "pipe", pairs)
    grad_query, grad_keyval = mirror_sum(
        own_q, far_q, own_kv, far_kv, [input_set], width
    )
    return attn_out, grad_input[None, None], grad_query[None], grad_keyval[None, :, None]


def solution(mesh):
    return jax.shard_map(
        on_device,
        mesh=mesh,
        in_specs=(
            P("pipe", "dp", "tensor", None),
            P(None, "dp"),
            P("pipe", "dp", None),
            P("pipe", "dp", "tensor", None),
            P("pipe", "dp", "tensor", None, None),
            P("pipe", "dp", None, "tensor", None),
        ),
        out_specs=(
            P("pipe", "dp", None, "tensor", None),
            P("pipe", "dp", "tensor", None),
            P("pipe", "dp", "tensor", None),
            P("pipe", "dp", "tensor", None, None),
        ),
        check_vma=False,
    )
```

```python
import functools
import math

import jax
import jax.numpy as jnp
from jax import lax
from jax.experimental import pallas as pl
from jax.experimental.pallas import tpu as pltpu
from jax.sharding import PartitionSpec as P

BF = jnp.bfloat16
F32 = jnp.float32
GROUP = 128
TOKEN = jax.ShapeDtypeStruct((8, 128), jnp.float32)
LIGHT = pl.CostEstimate(flops=1, bytes_accessed=1, transcendentals=0)
VM = pl.BlockSpec(memory_space=pltpu.VMEM)


def sin_turns(r):
    a = jnp.abs(r)
    m = jnp.minimum(a, 0.5 - a)
    x = (2.0 * math.pi) * m
    y = x * x
    p = -1.0 / 39916800.0
    p = p * y + 1.0 / 362880.0
    p = p * y - 1.0 / 5040.0
    p = p * y + 1.0 / 120.0
    p = p * y - 1.0 / 6.0
    s = x + x * (y * p)
    return jnp.where(r < 0, -s, s)


def quantize_block(w):
    top = jnp.max(jnp.abs(w), axis=0, keepdims=True)
    scale = (top + 1e-06) / 7.0
    t = w * (1.0 / scale)
    wave = sin_turns(t - jnp.round(t))
    return scale * (t - wave * (1.0 / (2.0 * math.pi)))


def quantize_kernel(wq_ref, wkv_ref, out_ref):
    columns = wq_ref.shape[1]
    out_ref[:, :columns] = quantize_block(wq_ref[...].astype(F32)).astype(BF)
    out_ref[:, columns:] = quantize_block(wkv_ref[...].astype(F32)).astype(BF)


def quantize(w_query, w_keyval):
    rows, q_cols = w_query.shape
    kv_cols = w_keyval.shape[1]
    cols = q_cols + kv_cols
    return pl.pallas_call(
        quantize_kernel,
        grid=(rows // GROUP,),
        in_specs=[
            pl.BlockSpec((GROUP, q_cols), lambda i: (i, 0)),
            pl.BlockSpec((GROUP, kv_cols), lambda i: (i, 0)),
        ],
        out_specs=pl.BlockSpec((GROUP, cols), lambda i: (i, 0)),
        out_shape=jax.ShapeDtypeStruct((rows, cols), BF),
        compiler_params=pltpu.CompilerParams(vmem_limit_bytes=4 * 2**20),
        cost_estimate=LIGHT,
    )(w_query, w_keyval)


def dot(a, b, dims):
    return lax.dot_general(a, b, (dims, ((), ())), preferred_element_type=F32)


def whole(shape):
    return pl.BlockSpec(shape, lambda *_: (0,) * len(shape))


def copy_kernel(moves, count, *refs):
    sems = refs[-1]
    copies = []
    for n, (source, take, target, put) in enumerate(moves):
        copies.append(
            pltpu.make_async_copy(
                refs[source].at[take], refs[count + target].at[put], sems.at[n]
            )
        )
    for copy in copies:
        copy.start()
    for copy in copies:
        copy.wait()


def copied(inputs, specs, after, moves, shapes):
    count = len(inputs) + len(after)
    return pl.pallas_call(
        functools.partial(copy_kernel, moves, count),
        grid=(1,),
        in_specs=specs + [pl.BlockSpec(memory_space=pl.ANY)] * len(after),
        out_specs=[pl.BlockSpec(memory_space=pltpu.HBM)] * len(shapes),
        out_shape=[jax.ShapeDtypeStruct(shape, BF) for shape in shapes],
        scratch_shapes=[pltpu.SemaphoreType.DMA((len(moves),))],
        compiler_params=pltpu.CompilerParams(vmem_limit_bytes=8 * 2**20),
        cost_estimate=LIGHT,
    )(*inputs, *after)


def halves(first, second, after, both):
    rows, cols = first.shape
    half = rows // 2
    top = (slice(0, half), slice(0, cols))
    if both:
        every = (slice(0, rows), slice(0, cols))
        bottom = (slice(half, rows), slice(0, cols))
        specs = [whole(first.shape), whole(second.shape)]
        rest = (slice(rows, 2 * rows), slice(0, cols))
        moves = [(0, top, 0, top), (1, bottom, 1, top), (0, every, 2, every), (1, every, 2, rest)]
        shapes = [(half, cols)] * 2 + [(2 * rows, cols)]
    else:
        specs = [
            pl.BlockSpec((half, cols), lambda i: (0, 0)),
            pl.BlockSpec((half, cols), lambda i: (1, 0)),
        ]
        moves = [(0, top, 0, top), (1, top, 1, top)]
        shapes = [(half, cols)] * 2
    return copied([first, second], specs, after, moves, shapes)


def pack_near(tokens, cols, rows):
    count = tokens[0].shape[1] // cols - 1
    moves = []
    for block in range(count):
        row = 0
        for n, part in enumerate(tokens):
            size = part.shape[0]
            take = (slice(0, size), slice((block + 1) * cols, (block + 2) * cols))
            moves.append((n, take, block, (slice(row, row + size), slice(0, cols))))
            row += size
    specs = [whole(t.shape) for t in tokens]
    return copied(tokens, specs, [], moves, [(rows, cols)] * count)


def pack_kernel(moves, parts, blocks, *refs):
    tokens, outs, sems = refs[:parts], refs[-2 - blocks : -1], refs[-1]
    copies = []
    for n, (source, take, target, put) in enumerate(moves):
        copies.append(
            pltpu.make_async_copy(tokens[source].at[take], outs[target].at[put], sems.at[n])
        )
    for copy in copies:
        copy.start()
    for copy in copies:
        copy.wait()


def pack_rest(tokens, blocks, after):
    rows, cols = blocks[0].shape
    count = len(blocks)
    model = tokens[0].shape[1]
    total = sum(t.shape[0] for t in tokens)
    moves, row = [], 0
    for n, part in enumerate(tokens):
        size = part.shape[0]
        for block in range(count):
            take = (slice(0, size), slice((block + 1) * cols, (block + 2) * cols))
            put = (slice(rows - total + row, rows - total + row + size), slice(0, cols))
            moves.append((n, take, block, put))
        every = (slice(0, size), slice(0, model))
        moves.append((n, every, count, (slice(row, row + size), slice(0, model))))
        row += size
    anywhere = pl.BlockSpec(memory_space=pl.ANY)
    return pl.pallas_call(
        functools.partial(pack_kernel, moves, len(tokens), count),
        grid=(1,),
        in_specs=[whole(t.shape) for t in tokens] + [anywhere] * (count + len(after)),
        out_specs=[anywhere] * (count + 1),
        out_shape=[jax.ShapeDtypeStruct((rows, cols), BF)] * count
        + [jax.ShapeDtypeStruct((total, model), BF)],
        input_output_aliases={len(tokens) + i: i for i in range(count)},
        scratch_shapes=[pltpu.SemaphoreType.DMA((len(moves),))],
        compiler_params=pltpu.CompilerParams(vmem_limit_bytes=8 * 2**20),
        cost_estimate=LIGHT,
    )(*tokens, *blocks, *after)


def relay_kernel(place_ref, fresh_ref, below_ref, above_ref, *rest):
    out_ref = rest[-1]
    source = place_ref[1]

    @pl.when(source == 0)
    def _():
        out_ref[...] = fresh_ref[...]

    @pl.when(source == 1)
    def _():
        out_ref[...] = below_ref[...]

    @pl.when(source == 2)
    def _():
        out_ref[...] = above_ref[...]


def relay(place, blocks, fresh, below, above, after):
    rows, model = fresh.shape
    tile = model // blocks
    source = pl.BlockSpec((rows, tile), lambda j, s: (0, (j + s[0]) % blocks))
    return pl.pallas_call(
        relay_kernel,
        grid_spec=pltpu.PrefetchScalarGridSpec(
            num_scalar_prefetch=1,
            grid=(blocks,),
            in_specs=[source] * 3 + [pl.BlockSpec(memory_space=pl.ANY)] * len(after),
            out_specs=pl.BlockSpec((rows, tile), lambda j, s: (0, j)),
        ),
        out_shape=jax.ShapeDtypeStruct((rows, model), BF),
        compiler_params=pltpu.CompilerParams(vmem_limit_bytes=4 * 2**20),
        cost_estimate=LIGHT,
    )(place, fresh, below, above, *after)


def gather_kernel(place_ref, in_ref, out_ref, token_ref):
    token_ref[...] = jnp.zeros_like(token_ref)
    width = in_ref.shape[2]
    for i in range(in_ref.shape[1]):
        out_ref[:, i * width : (i + 1) * width] = in_ref[:, i, :]


def gather_rows(place, value):
    rows, heads, width = value.shape
    count = place.shape[0]
    tile = rows // count
    return pl.pallas_call(
        gather_kernel,
        grid_spec=pltpu.PrefetchScalarGridSpec(
            num_scalar_prefetch=1,
            grid=(count,),
            in_specs=[pl.BlockSpec((tile, heads, width), lambda i, s: (s[i], 0, 0))],
            out_specs=[
                pl.BlockSpec((tile, heads * width), lambda i, s: (i, 0)),
                whole(TOKEN.shape),
            ],
        ),
        out_shape=[jax.ShapeDtypeStruct((rows, heads * width), value.dtype), TOKEN],
        compiler_params=pltpu.CompilerParams(vmem_limit_bytes=4 * 2**20),
        cost_estimate=LIGHT,
    )(place, value)


def scatter_kernel(place_ref, in_ref, after_ref, out_ref, token_ref):
    token_ref[...] = jnp.zeros_like(token_ref)
    width = out_ref.shape[2]
    for i in range(out_ref.shape[1]):
        out_ref[:, i, :] = in_ref[:, i * width : (i + 1) * width]


def scatter_rows(place, value, width, after):
    rows, cols = value.shape
    heads = cols // width
    count = place.shape[0]
    tile = rows // count
    return pl.pallas_call(
        scatter_kernel,
        grid_spec=pltpu.PrefetchScalarGridSpec(
            num_scalar_prefetch=1,
            grid=(count,),
            in_specs=[
                pl.BlockSpec((tile, cols), lambda i, s: (i, 0)),
                pl.BlockSpec(memory_space=pl.ANY),
            ],
            out_specs=[
                pl.BlockSpec((tile, heads, width), lambda i, s: (s[i], 0, 0)),
                whole(TOKEN.shape),
            ],
        ),
        out_shape=[jax.ShapeDtypeStruct((rows, heads, width), value.dtype), TOKEN],
        compiler_params=pltpu.CompilerParams(vmem_limit_bytes=4 * 2**20),
        cost_estimate=LIGHT,
    )(place, value, after)


def first_half(value):
    return pl.BlockSpec((value.shape[0] // 2, value.shape[1]), lambda i: (0, 0))


def half_of(value):
    return jax.ShapeDtypeStruct((value.shape[0] // 2, value.shape[1]), value.dtype)


def second_step_kernel(up_ref, down_ref, next_ref, prev_ref, *rest):
    up_out, down_out, token_ref = rest[-3:]
    token_ref[...] = jnp.zeros_like(token_ref)
    up_out[...] = (up_ref[...].astype(F32) + next_ref[...].astype(F32)).astype(BF)
    down_out[...] = (down_ref[...].astype(F32) + prev_ref[...].astype(F32)).astype(BF)


def second_step(up, down, next_top, prev_bot, after):
    outs = [half_of(up), half_of(down), TOKEN]
    return pl.pallas_call(
        second_step_kernel,
        grid=(1,),
        in_specs=[first_half(up), first_half(down)]
        + [whole(next_top.shape), whole(prev_bot.shape)]
        + [pl.BlockSpec(memory_space=pl.ANY)] * len(after),
        out_specs=[whole(o.shape) for o in outs],
        out_shape=outs,
        compiler_params=pltpu.CompilerParams(vmem_limit_bytes=4 * 2**20),
        cost_estimate=pl.CostEstimate(
            flops=8 * 10**9, bytes_accessed=1, transcendentals=0
        ),
    )(up, down, next_top, prev_bot, *after)


def input_grad_kernel(
    shift_ref, kept_ref, up_ref, down_ref, up2_ref, down2_ref, out_ref, token_ref
):
    token_ref[...] = jnp.zeros_like(token_ref)
    half = up2_ref.shape[0]
    total = kept_ref[...].astype(F32)
    bottom = total[half:] + up_ref[...].astype(F32) + down2_ref[...].astype(F32)
    top = total[:half] + up2_ref[...].astype(F32) + down_ref[...].astype(F32)
    out_ref[:half, :] = top.astype(BF)
    out_ref[half:, :] = bottom.astype(BF)


def input_grad(replica, replicas, kept, up, down, up2, down2):
    rows, model = kept.shape
    tile = model // replicas
    part = lambda r, k: pl.BlockSpec((r, tile), lambda j, s: (k, j))
    return pl.pallas_call(
        input_grad_kernel,
        grid_spec=pltpu.PrefetchScalarGridSpec(
            num_scalar_prefetch=1,
            grid=(replicas,),
            in_specs=[
                part(rows, 0),
                part(rows // 2, 1),
                part(rows // 2, 1),
                part(rows // 2, 0),
                part(rows // 2, 0),
            ],
            out_specs=[
                pl.BlockSpec((rows, tile), lambda j, s: (0, (j + s[0]) % replicas)),
                whole(TOKEN.shape),
            ],
        ),
        out_shape=[jax.ShapeDtypeStruct((rows, model), BF), TOKEN],
        compiler_params=pltpu.CompilerParams(vmem_limit_bytes=4 * 2**20),
        cost_estimate=pl.CostEstimate(
            flops=40 * 10**9, bytes_accessed=160 * 2**20, transcendentals=0
        ),
    )(replica.reshape(1), kept, up, down, up2, down2)


def project_kernel(parts, *refs):
    tokens, weights = refs[:parts], refs[parts:-3]
    out_ref, first_ref, held = refs[-3:]

    @pl.when(pl.program_id(0) == 0)
    def _():
        row = 0
        for ref in tokens:
            held[row : row + ref.shape[0], :] = ref[...]
            row += ref.shape[0]
        first_ref[...] = held[:, : first_ref.shape[1]]

    total, at = None, 0
    for ref in weights:
        term = dot(held[:, at : at + ref.shape[0]], ref[...], ((1,), (0,)))
        total = term if total is None else total + term
        at += ref.shape[0]
    out_ref[...] = total.astype(BF)


def project(tokens, weights, first):
    rows = sum(t.shape[0] for t in tokens)
    model = tokens[0].shape[1]
    cols = weights[0].shape[1]
    tile = 256
    return pl.pallas_call(
        functools.partial(project_kernel, len(tokens)),
        grid=(cols // tile,),
        in_specs=[whole(t.shape) for t in tokens]
        + [pl.BlockSpec((w.shape[0], tile), lambda i: (0, i)) for w in weights],
        out_specs=[pl.BlockSpec((rows, tile), lambda i: (0, i)), whole((rows, first))],
        out_shape=[
            jax.ShapeDtypeStruct((rows, cols), BF),
            jax.ShapeDtypeStruct((rows, first), BF),
        ],
        scratch_shapes=[pltpu.VMEM((rows, model), BF)],
        compiler_params=pltpu.CompilerParams(vmem_limit_bytes=28 * 2**20),
        cost_estimate=LIGHT,
    )(*tokens, *weights)


def attention_kernel(
    q_ref, kv_ref, cos_ref, sin_ref, pos_row_ref, pos_col_ref, og_ref,
    out_ref, d_ref, k_rot, dk_sum, dv_sum,
):
    width = cos_ref.shape[1]
    half = width // 2
    head = pl.program_id(0)
    heads = pl.num_programs(0)
    cosine = cos_ref[...]
    signed = sin_ref[...]

    @pl.when(head == 0)
    def _():
        k = kv_ref[:, :width].astype(F32)
        k_rot[...] = (k * cosine + pltpu.roll(k, half, 1) * signed).astype(BF)
        dk_sum[...] = jnp.zeros_like(dk_sum)
        dv_sum[...] = jnp.zeros_like(dv_sum)

    values = kv_ref[:, width:]
    keys = k_rot[...]
    q = q_ref[...].astype(F32)
    q_rot = (q * cosine + pltpu.roll(q, half, 1) * signed).astype(BF)
    factor = 1.0 / math.sqrt(width)
    scores = dot(q_rot, keys, ((1,), (1,)))
    visible = pos_row_ref[...] <= pos_col_ref[...]
    scores = jnp.where(visible, scores, -1e30)
    raised = jnp.exp2(
        (scores - jnp.max(scores, axis=1, keepdims=True)) * (factor * math.log2(math.e))
    )
    weights = raised * (1.0 / jnp.sum(raised, axis=1, keepdims=True))
    weights_low = weights.astype(BF)
    out_ref[...] = dot(weights_low, values, ((1,), (0,))).astype(BF)
    cotangent = og_ref[...]
    dv_sum[...] += dot(weights_low, cotangent, ((0,), (0,)))
    d_weights = dot(cotangent, values, ((1,), (1,)))
    delta = jnp.sum(d_weights * weights, axis=1, keepdims=True)
    d_scores = (weights * (d_weights - delta)).astype(BF)
    dq = dot(d_scores, keys, ((1,), (0,))) * factor
    dk_sum[...] += dot(d_scores, q_rot, ((0,), (0,)))
    place = pl.ds(pl.multiple_of(head * width, width), width)
    d_ref[:, place] = (dq * cosine + pltpu.roll(dq * signed, half, 1)).astype(BF)

    @pl.when(head == heads - 1)
    def _():
        dk = dk_sum[...] * factor
        q_cols = d_ref.shape[1] - 2 * width
        dk = (dk * cosine + pltpu.roll(dk * signed, half, 1)).astype(BF)
        d_ref[:, q_cols : q_cols + width] = dk
        d_ref[:, q_cols + width :] = dv_sum[...].astype(BF)


def attention(projected, heads, width, cos_t, sin_t, positions, out_grad):
    length, cols = projected.shape
    q_cols = heads * width
    column = pl.BlockSpec((length, width), lambda h: (0, h))
    return pl.pallas_call(
        attention_kernel,
        grid=(heads,),
        in_specs=[
            column,
            pl.BlockSpec((length, 2 * width), lambda h: (0, heads // 2)),
            whole((length, width)),
            whole((length, width)),
            whole((1, length)),
            whole((length, 1)),
            column,
        ],
        out_specs=[column, whole((length, cols))],
        out_shape=[
            jax.ShapeDtypeStruct((length, q_cols), BF),
            jax.ShapeDtypeStruct((length, cols), BF),
        ],
        scratch_shapes=[
            pltpu.VMEM((length, width), BF),
            pltpu.VMEM((length, width), F32),
            pltpu.VMEM((length, width), F32),
        ],
        compiler_params=pltpu.CompilerParams(vmem_limit_bytes=16 * 2**20),
        cost_estimate=LIGHT,
    )(projected, projected, cos_t, sin_t, positions[None, :], positions[:, None], out_grad)


def partial_kernel(parts, *refs):
    weights, (own_ref, other_ref, held, sems) = refs[1 : 1 + parts], refs[-4:]
    copies, at = [], 0
    for n, ref in enumerate(weights):
        size = ref.shape[0]
        copies.append(pltpu.make_async_copy(ref, held.at[at : at + size, :], sems.at[n]))
        at += size
    for copy in copies:
        copy.start()
    grads = refs[0][...]
    near = own_ref.shape[0]
    at = 0
    for copy, ref in zip(copies, weights):
        columns = slice(at, at + ref.shape[0])
        copy.wait()
        total = dot(grads, held[columns, :], ((1,), (1,))).astype(BF)
        own_ref[:, columns] = total[:near]
        other_ref[:, columns] = total[near:]
        at += ref.shape[0]


def partial(grads, weights, after):
    rows, cols = grads.shape
    model = sum(w.shape[0] for w in weights)
    anywhere = pl.BlockSpec(memory_space=pl.ANY)
    return pl.pallas_call(
        functools.partial(partial_kernel, len(weights)),
        in_specs=[VM] + [anywhere] * (len(weights) + len(after)),
        out_specs=[VM, VM],
        out_shape=[jax.ShapeDtypeStruct((rows // 2, model), BF)] * 2,
        scratch_shapes=[
            pltpu.VMEM((model, cols), BF),
            pltpu.SemaphoreType.DMA((len(weights),)),
        ],
        compiler_params=pltpu.CompilerParams(vmem_limit_bytes=16 * 2**20),
        cost_estimate=LIGHT,
    )(grads, *weights, *after)


def chip_sum_kernel(cuts, a_ref, b_ref, *rest):
    outs = rest[-1 - len(cuts) : -1]
    rest[-1][...] = jnp.zeros_like(rest[-1])
    for out, ranges in zip(outs, cuts):
        row = 0
        for low, high in ranges:
            total = a_ref[low:high, :].astype(F32) + b_ref[low:high, :].astype(F32)
            out[row : row + high - low, :] = total.astype(BF)
            row += high - low


def chip_sum(a, b, cuts, after):
    rows, model = a.shape
    tile = model // 4
    sizes = [sum(high - low for low, high in ranges) for ranges in cuts]
    block = lambda r: pl.BlockSpec((r, tile), lambda j: (0, j))
    return pl.pallas_call(
        functools.partial(chip_sum_kernel, cuts),
        grid=(model // tile,),
        in_specs=[block(rows)] * 2 + [pl.BlockSpec(memory_space=pl.ANY)] * len(after),
        out_specs=[block(size) for size in sizes] + [whole(TOKEN.shape)],
        out_shape=[jax.ShapeDtypeStruct((size, model), BF) for size in sizes] + [TOKEN],
        compiler_params=pltpu.CompilerParams(vmem_limit_bytes=6 * 2**20),
        cost_estimate=LIGHT,
    )(a, b, *after)


def weight_grad_kernel(count, first, *refs):
    tokens, grads, rest = refs[:count], refs[count : 2 * count], refs[2 * count :]
    rest = rest[-2:] if first else rest[:1] + rest[-2:]
    total = None if first else rest[0][...]
    for x, d in zip(tokens, grads):
        term = dot(x[...], d[...], ((0,), (0,)))
        total = term if total is None else total + term
    if first:
        rest[0][...] = total
        rest[1][...] = jnp.zeros_like(rest[1])
    else:
        q_ref, kv_ref = rest[1:]
        q_cols = q_ref.shape[1]
        q_ref[...] = total[:, :q_cols].astype(BF)
        kv_ref[...] = total[:, q_cols:].astype(BF)


def weight_grad(tokens, grads, sums, q_cols, after=()):
    count = len(tokens)
    d_rows = tokens[0].shape[1]
    cols = grads[0][0].shape[1]
    tile = 256
    block = lambda width: pl.BlockSpec((tile, width), lambda i: (i, 0))
    in_specs = [pl.BlockSpec((t.shape[0], tile), lambda i: (0, i)) for t in tokens]
    for grad, part in grads:
        if part is None:
            in_specs.append(whole(grad.shape))
        else:
            shape = (grad.shape[0] // 2, cols)
            in_specs.append(pl.BlockSpec(shape, functools.partial(lambda p, i: (p, 0), part)))
    if sums is None:
        operands = tuple(after)
        in_specs += [pl.BlockSpec(memory_space=pl.ANY)] * len(after)
        out_specs = [block(cols), whole(TOKEN.shape)]
        out_shape = [jax.ShapeDtypeStruct((d_rows, cols), F32), TOKEN]
    else:
        operands = (sums,) + tuple(after)
        in_specs.append(block(cols))
        in_specs += [pl.BlockSpec(memory_space=pl.ANY)] * len(after)
        out_specs = [block(q_cols), block(cols - q_cols)]
        out_shape = [
            jax.ShapeDtypeStruct((d_rows, q_cols), BF),
            jax.ShapeDtypeStruct((d_rows, cols - q_cols), BF),
        ]
    return pl.pallas_call(
        functools.partial(weight_grad_kernel, count, sums is None),
        grid=(d_rows // tile,),
        in_specs=in_specs,
        out_specs=out_specs,
        out_shape=out_shape,
        compiler_params=pltpu.CompilerParams(vmem_limit_bytes=13 * 2**20),
        cost_estimate=LIGHT,
    )(*tokens, *[g for g, _ in grads], *operands)


def mirror_sum_kernel(q_ref, q_far_ref, kv_ref, kv_far_ref, *rest):
    out_q_ref, out_kv_ref = rest[-2:]
    width = out_q_ref.shape[-1]
    q = q_ref[...].astype(F32) + q_far_ref[...].astype(F32)
    kv = kv_ref[...].astype(F32) + kv_far_ref[...].astype(F32)
    for i in range(out_q_ref.shape[1]):
        out_q_ref[:, i, :] = q[:, i * width : (i + 1) * width]
    for i in range(out_kv_ref.shape[1]):
        out_kv_ref[:, i, :] = kv[:, i * width : (i + 1) * width]


def mirror_sum(q, q_far, kv, kv_far, after, width):
    rows, q_cols = q.shape
    kv_cols = kv.shape[1]
    tile = 256
    flat = lambda cols: pl.BlockSpec((tile, cols), lambda i: (i, 0))
    deep = lambda cols: pl.BlockSpec((tile, cols // width, width), lambda i: (i, 0, 0))
    return pl.pallas_call(
        mirror_sum_kernel,
        grid=(rows // tile,),
        in_specs=[flat(q_cols), flat(q_cols), flat(kv_cols), flat(kv_cols)]
        + [pl.BlockSpec(memory_space=pl.ANY)] * len(after),
        out_specs=[deep(q_cols), deep(kv_cols)],
        out_shape=[
            jax.ShapeDtypeStruct((rows, q_cols // width, width), F32),
            jax.ShapeDtypeStruct((rows, kv_cols // width, width), F32),
        ],
        compiler_params=pltpu.CompilerParams(vmem_limit_bytes=6 * 2**20),
        cost_estimate=LIGHT,
    )(q, q_far, kv, kv_far, *after)


def shifted(value, axis, step):
    count = lax.axis_size(axis)
    return lax.ppermute(value, axis, [(i, (i + step) % count) for i in range(count)])


def shifted_chips(value, step):
    count = lax.axis_size("tensor")
    chips = count // 2
    pairs = [(i, ((i // 2 + step) % chips) * 2 + i % 2) for i in range(count)]
    return lax.ppermute(value, "tensor", pairs)


def other_core(value):
    return lax.ppermute(value, "tensor", [(i, i ^ 1) for i in range(lax.axis_size("tensor"))])


def roll_blocks(value, axis, shift, count):
    block = value.shape[axis] // count
    doubled = jnp.concatenate([value, value], axis=axis)
    return lax.dynamic_slice_in_dim(doubled, shift * block, value.shape[axis], axis=axis)


def on_device(act, direction, positions, w_query, w_keyval, out_grad):
    section = lax.axis_index("pipe")
    sections = lax.axis_size("pipe")
    tensor = lax.axis_index("tensor")
    chip, core = tensor // 2, tensor % 2
    chips = lax.axis_size("tensor") // 2
    replica = lax.axis_index("dp")
    replicas = lax.axis_size("dp")
    d_rows, heads, width = w_query.shape[1:]
    seq_len = positions.shape[2]
    q_cols = heads * width
    piece = act.shape[2]
    near = seq_len // 2
    half = piece // 2

    fresh = act[0, 0]
    ends = sections - 1
    from_below = lax.ppermute(fresh, "pipe", [(i, i + 1) for i in range(ends)])
    from_above = lax.ppermute(fresh, "pipe", [(i + 1, i) for i in range(ends)])

    w_own = quantize(w_query[0].reshape(d_rows, -1), w_keyval[0].reshape(d_rows, -1))
    w_before = shifted(w_own, "dp", 1)
    w_after = shifted(w_own, "dp", -1)

    heading = lax.dynamic_index_in_dim(direction, section, 0, keepdims=False)[0]
    source = jnp.where(
        heading == 0, jnp.where(section == 0, 0, 1), jnp.where(section == ends, 0, 2)
    )
    order = jnp.array([0, 1, chips - 1, 2], jnp.int32)
    order = (chip + order) % chips
    place = jnp.concatenate([order * 2 + core, order * 2 + 1 - core])
    pos = jnp.take(positions[0, 0].reshape(-1, piece), place, axis=0).reshape(-1)
    cotangent, rows_set = gather_rows(place, out_grad[0, 0])
    angle_half = width // 2
    inv_freq = 1000000.0 ** (-jnp.arange(angle_half, dtype=F32) / angle_half)
    angles = pos.astype(F32)[:, None] * inv_freq[None, :]
    cosine, sine = jnp.cos(angles), jnp.sin(angles)
    cos_t = jnp.concatenate([cosine, cosine], axis=1)
    sin_t = jnp.concatenate([-sine, sine], axis=1)
    own = relay(
        jnp.stack([replica, source]),
        replicas,
        fresh,
        from_below,
        from_above,
        [w_own, cos_t, sin_t, rows_set],
    )
    prev = shifted_chips(own, 1)
    after = shifted_chips(own, -1)

    other_own = other_core(own)
    before_top, after_bot = halves(w_before, w_after, [other_own], False)
    next_top, prev_bot, beside = halves(after, prev, [before_top], True)
    far_top = shifted(before_top, "dp", 1)
    far_bot = shifted(after_bot, "dp", -1)
    across_top = shifted_chips(next_top, -1)
    across_bot = shifted_chips(prev_bot, 1)

    blocks = pack_near([own, beside], d_rows, near)
    *blocks, across = pack_rest([across_top, across_bot], blocks, [far_top, far_bot])
    sent = [shifted(blocks[k - 1], "dp", k) for k in range(1, replicas)]
    token_parts = [own, beside, across]
    other_parts = [other_own, other_core(beside), other_core(across)]

    weights = [w_own, w_after, far_top, far_bot, w_before]
    projected, x_own = project(token_parts + other_parts, weights, d_rows)
    attended, d_own = attention(projected, heads, width, cos_t, sin_t, pos, cotangent)

    own_part, other_part = partial(d_own, weights, sent)
    other_part = other_core(other_part)
    sent_other = [other_core(x) for x in sent]
    low = [i * piece for i in range(chips)]
    mid = [i * piece + half for i in range(chips)]
    high = [(i + 1) * piece for i in range(chips)]
    kept, up, next_top, down, prev_bot, chip_set = chip_sum(
        own_part,
        other_part,
        [
            [(low[0], high[0])],
            [(low[3], mid[3]), (mid[1], high[1])],
            [(low[1], mid[1])],
            [(mid[3], high[3]), (low[2], mid[2])],
            [(mid[2], high[2])],
        ],
        [],
    )
    up = shifted_chips(up, 1)
    down = shifted_chips(down, -1)

    d_before = shifted(d_own, "dp", 1)
    d_after = shifted(d_own, "dp", -1)
    before_top, after_bot = halves(
        d_before, d_after, [chip_set] + sent_other, False
    )
    d_far_top = shifted(before_top, "dp", 1)
    d_far_bot = shifted(after_bot, "dp", -1)
    attn_out, out_set = scatter_rows(place, attended, width, chip_set)
    attn_out = attn_out[None, None]
    sums, sums_set = weight_grad(
        [x_own, sent[0], sent_other[0], sent[2], sent_other[2]],
        [(d_own, None), (d_before, 0), (d_before, 1), (d_after, 0), (d_after, 1)],
        None,
        q_cols,
        [chip_set, out_set],
    )
    up2_part, down2_part, step_set = second_step(
        up, down, next_top, prev_bot, [sums_set, out_set]
    )
    up2 = shifted_chips(up2_part, 1)
    down2 = shifted_chips(down2_part, -1)
    grad_input, input_set = input_grad(replica, replicas, kept, up, down, up2, down2)
    own_q, own_kv = weight_grad(
        [sent[1], sent_other[1]], [(d_far_top, None), (d_far_bot, None)], sums, q_cols, [step_set]
    )
    pairs = [(i, ends - i) for i in range(sections)]
    far_q = lax.ppermute(own_q, "pipe", pairs)
    far_kv = lax.ppermute(own_kv, "pipe", pairs)
    grad_query, grad_keyval = mirror_sum(
        own_q, far_q, own_kv, far_kv, [input_set], width
    )
    return attn_out, grad_input[None, None], grad_query[None], grad_keyval[None, :, None]


def solution(mesh):
    return jax.shard_map(
        on_device,
        mesh=mesh,
        in_specs=(
            P("pipe", "dp", "tensor", None),
            P(None, "dp"),
            P("pipe", "dp", None),
            P("pipe", "dp", "tensor", None),
            P("pipe", "dp", "tensor", None, None),
            P("pipe", "dp", None, "tensor", None),
        ),
        out_specs=(
            P("pipe", "dp", None, "tensor", None),
            P("pipe", "dp", "tensor", None),
            P("pipe", "dp", "tensor", None),
            P("pipe", "dp", "tensor", None, None),
        ),
        check_vma=False,
    )
```
